32 devices in a mesh: dp: 4 (over x, core), fsdp: 8 (over z, y).
Axes of the slice: x: 2, y: 2, z: 4, core: 2. Of those that a mesh axis runs over, the one named last changes fastest.
Arguments:
- layer_input: bfloat16 [376832, 512], P(('dp', 'fsdp')), may hold values from -6 to 6
- cotangent: bfloat16 [376832, 512], P(('dp', 'fsdp')), may hold values from -6 to 6
- shape_points: int32 [64], replicated, may hold values from 1 to 11776, 376832 in all
- shape_category: int32 [64], replicated, may hold values from 0 to 12
- category_counts: int32 [13], replicated, may hold values from 1 to 8
- dir_a: bfloat16 [512, 512], P(('dp', 'fsdp')), may hold values from -0.25 to 0.25
- gain_a: bfloat16 [512], P(('dp', 'fsdp')), may hold values from 0.5 to 1.5
- bias_a: bfloat16 [512], P(('dp', 'fsdp')), may hold values from -1.5 to 1.5
- dir_b: bfloat16 [512, 512], P(('dp', 'fsdp')), may hold values from -0.25 to 0.25
- gain_b: bfloat16 [512], P(('dp', 'fsdp')), may hold values from 0.5 to 1.5
- bias_b: bfloat16 [512], P(('dp', 'fsdp')), may hold values from -1.5 to 1.5
Outputs:
- layer_output: bfloat16 [376832, 512], P(('dp', 'fsdp'))
- input_grad: bfloat16 [376832, 512], P(('dp', 'fsdp'))
- dir_a_grad: float32 [512, 512], P(('dp', 'fsdp'))
- gain_a_grad: float32 [512], P(('dp', 'fsdp'))
- bias_a_grad: float32 [512], P(('dp', 'fsdp'))
- dir_b_grad: float32 [512, 512], P(('dp', 'fsdp'))
- gain_b_grad: float32 [512], P(('dp', 'fsdp'))
- bias_b_grad: float32 [512], P(('dp', 'fsdp'))
The draws below stay inside these ranges and needn't reach their ends.
Inputs may be any that keep to these rules, and one draw needn't show every extreme that they name: `shape_points`: sums to 376832; the largest shape has exactly 11776 points.
All inputs are finite; a program needn't handle non-finite values.
Results may differ from the reference program's by a relative error of at most 0.0079.
Values may be sent and summed in bfloat16 or wider, within the bound.
No kernel may reach another device: no remote copies, remote signals or barrier semaphores. Data moves between devices by JAX's collectives and lax.ppermute only.
A program may use at most 256 MiB of HBM per device.

```python
import math
import jax
import jax.numpy as jnp
import numpy as np
from jax import lax

WIDTH = 512
CATS = 13
PTS_DEV = 11776
POINTS = 376832
SHAPES = 64
MOST = 11776
DEVICES = 32


def set_ends(entries, rng, low, largest):
    longest = entries.shape.index(max(entries.shape))
    spots = []
    for shift in (0, 1):
        where = [jax.random.randint(jax.random.fold_in(rng, axis), (), 0, length) for axis, length in enumerate(entries.shape)]
        where[longest] = (where[longest] + shift) % entries.shape[longest]
        spots.append(tuple(where))
    return entries.at[spots[0]].set(low).at[spots[1]].set(largest)


def raised(entries, stream_key, source, target, shards_of, factor):
    owner, partner = [(jnp.arange(entries.shape[dim]) // (entries.shape[dim] // shards_of)).reshape([-1 if axis == dim else 1 for axis in range(entries.ndim)]) for dim in (source, target)]
    chosen = jax.random.permutation(stream_key, shards_of)[partner]
    strong = (owner == chosen) | (owner == (partner + shards_of // 2) % shards_of)
    return jnp.where(strong, factor * entries, entries)


def level_of(rng, dims, shards, smallest, largest):
    factor_of = 1.0
    for dim, blocks in shards:
        heights = jax.random.uniform(jax.random.fold_in(jax.random.fold_in(rng, 6), dim), (blocks,), jnp.float32, smallest / len(shards), largest / len(shards))
        factor_of = factor_of * jnp.repeat(jnp.exp(heights), dims[dim] // blocks).reshape((-1,) + (1,) * (len(dims) - 1 - dim))
    return factor_of


def length_profile(amount, total, limit, slope):
    weights = [(1 << 20) // math.isqrt(standing ** slope) + 1 for standing in range(2, amount + 1)]
    spare, given = total - limit - (amount - 1), [1] * (amount - 1)
    while spare > 0:
        candidates = [i for i in range(amount - 1) if given[i] < limit]
        mass, budget = sum([weights[i] for i in candidates]), spare
        for i in candidates:
            addition = min(limit - given[i], max(1, budget * weights[i] // mass), spare)
            given[i] = given[i] + addition
            spare = spare - addition
    return np.array([limit] + given)


def uneven_parts(stream_key, count, total, most, slope):
    if count == 2:
        one = jax.random.randint(stream_key, (), max(1, total - most), min(most, total - 1) + 1)
        return jnp.stack([one, total - one])
    sizes = jnp.asarray(length_profile(count, total, most, slope), jnp.int32)
    couples = (count - 1) // 2
    giver, taker = sizes[1:1 + 2 * couples:2], sizes[2:2 + 2 * couples:2]
    room = jnp.minimum(giver - 1, most - taker)
    moved = jax.random.randint(jax.random.fold_in(stream_key, 1), (couples,), 0, 1 << 20) % (room + 1)
    sizes = sizes.at[1:1 + 2 * couples:2].set(giver - moved).at[2:2 + 2 * couples:2].set(taker + moved)
    return sizes[jax.random.permutation(jax.random.fold_in(stream_key, 2), count)]


def centred(stream_key, dims, deviation, limit, split=(), held_as=jnp.bfloat16):
    drawn = jax.random.normal(stream_key, dims, jnp.float32) * deviation
    if len(split) > 0:
        drawn = level_of(stream_key, dims, split, -0.22, 0.18) * drawn
    return jnp.clip(drawn, min=-limit, max=limit).astype(held_as)


def gaussian_with(rng, extent, spread, limit, split, heavy, held_as=jnp.bfloat16):
    values = spread * jax.random.normal(rng, extent, jnp.float32)
    if split:
        values = values * level_of(rng, extent, split, -0.22, 0.18)
    return jnp.clip(raised(values, jax.random.fold_in(rng, 3), *heavy), -limit, limit).astype(held_as)


def setup_inputs(seed: int = 0) -> dict:
    seeds = jax.random.split(jax.random.key(seed), 12)
    return {
        "layer_input": gaussian_with(seeds[0], (POINTS, WIDTH), 1.0, 6.0, ((0, 32),), (0, 1, 32, 2.75)),
        "cotangent": centred(seeds[1], (POINTS, WIDTH), 1.0, 6.0, ((0, 32),)),
        "shape_points": uneven_parts(seeds[2], SHAPES, POINTS, MOST, 2).astype(jnp.int32),
        "shape_category": set_ends(jax.random.randint(seeds[3], (SHAPES,), 0, CATS), jax.random.fold_in(seeds[3], 1), 0, CATS - 1).astype(jnp.int32),
        "category_counts": set_ends(jax.random.randint(seeds[4], (CATS,), 1, 9), jax.random.fold_in(seeds[4], 1), 1, 8).astype(jnp.int32),
        "dir_a": centred(seeds[5], (WIDTH, WIDTH), WIDTH ** -0.5, 0.25, ((0, 32),)),
        "gain_a": jnp.clip(1.0 + 0.1 * jax.random.normal(seeds[6], (WIDTH,), jnp.float32), 0.5, 1.5).astype(jnp.bfloat16),
        "bias_a": centred(seeds[7], (WIDTH,), 0.3, 1.5, ((0, 32),)),
        "dir_b": centred(seeds[8], (WIDTH, WIDTH), WIDTH ** -0.5, 0.25, ((0, 32),)),
        "gain_b": jnp.clip(1.0 + 0.1 * jax.random.normal(seeds[9], (WIDTH,), jnp.float32), 0.5, 1.5).astype(jnp.bfloat16),
        "bias_b": centred(seeds[10], (WIDTH,), 0.3, 1.5, ((0, 32),)),
    }


@jax.custom_vjp
def low(v):
    return lax.optimization_barrier(v.astype(jnp.bfloat16)).astype(jnp.float32)

@jax.custom_vjp
def low_back(v):
    return v

def low_keep(v):
    return (low(v), None)

def low_pass(kept, grad):
    return (grad,)

def back_keep(v):
    return (v, None)

def back_low(kept, grad):
    return (low(grad),)
low.defvjp(low_keep, low_pass)
low_back.defvjp(back_keep, back_low)
EPS = 1e-06

def layer_weight(direction, gain):
    norm_inv = lax.rsqrt(lax.optimization_barrier(jnp.sum(direction * direction, axis=0)) + EPS)
    return low(gain * norm_inv * direction)

def block_rows(weight_a, bias_a, weight_b, bias_b, rows):
    pre_a = low_back(jnp.dot(rows, weight_a, precision=lax.Precision.HIGHEST) + bias_a)
    hidden = low(jax.nn.silu(pre_a))
    pre_b = low_back(jnp.dot(hidden, weight_b, precision=lax.Precision.HIGHEST) + bias_b)
    return jax.nn.silu(pre_b)

def forward(inputs, dir_a, gain_a, bias_a, dir_b, gain_b, bias_b):
    weight_a = layer_weight(dir_a, gain_a)
    weight_b = layer_weight(dir_b, gain_b)
    checked = jax.checkpoint(block_rows)

    def step(carry, rows):
        return (carry, checked(weight_a, bias_a, weight_b, bias_b, rows))
    carry, outputs = lax.scan(step, jnp.zeros((), jnp.float32), inputs)
    return outputs

def reference(layer_input, cotangent, shape_points, shape_category, category_counts, dir_a, gain_a, bias_a, dir_b, gain_b, bias_b):
    inputs = layer_input.astype(jnp.float32).reshape(DEVICES, PTS_DEV, WIDTH)
    params = [p.astype(jnp.float32) for p in (dir_a, gain_a, bias_a, dir_b, gain_b, bias_b)]
    outputs, pull = jax.vjp(forward, inputs, *params)
    average = POINTS // SHAPES
    counts = category_counts[shape_category].astype(jnp.float32)
    shape_weight = counts * (average / 4.0) / jnp.maximum(shape_points, average // 2).astype(jnp.float32)
    point_weight = jnp.repeat(shape_weight, shape_points, total_repeat_length=POINTS)
    weighted = cotangent.astype(jnp.float32).reshape(DEVICES, PTS_DEV, WIDTH) * point_weight.reshape(DEVICES, PTS_DEV, 1)
    grads = pull(weighted)
    layer_output = outputs.reshape(POINTS, WIDTH).astype(jnp.bfloat16)
    input_grad = grads[0].reshape(POINTS, WIDTH).astype(jnp.bfloat16)
    return (layer_output, input_grad, grads[1], grads[2], grads[3], grads[4], grads[5], grads[6])
```

```python
import functools

import jax
import jax.numpy as jnp
from jax import lax
from jax.experimental import pallas as pl
from jax.experimental.pallas import tpu as pltpu
from jax.sharding import PartitionSpec as P

AXES = ("dp", "fsdp")
EPS = 1e-06
SLOT = 16
LANES = 128
F32 = jnp.float32
BF16 = jnp.bfloat16
VMEM_BYTES = 60 << 20


def pick_tile(rows):
    for tile in (1472, 736, 512, 368, 256, 128, 64, 32, 16):
        if rows % tile == 0:
            return tile
    return rows


def dot(left, right):
    return jnp.dot(left, right, preferred_element_type=F32)


def point_weight_kernel(average, place_ref, counts_ref, points_ref, category_ref, out_ref, table):
    shapes = points_ref.shape[1]
    points = points_ref[...]
    lane = lax.broadcasted_iota(jnp.int32, points.shape, 1)
    ends = points
    shift = 1
    while shift < shapes:
        ends = ends + jnp.where(lane >= shift, pltpu.roll(ends, shift, 1), 0)
        shift *= 2
    starts = ends - points

    @pl.when(pl.program_id(0) == 0)
    def _():
        count = jnp.zeros(points.shape, jnp.int32)
        for cat in range(counts_ref.shape[0]):
            count = jnp.where(category_ref[...] == cat, counts_ref[cat], count)
        weight = (
            count.astype(F32) * (average / 4.0) / jnp.maximum(points, average // 2).astype(F32)
        )
        square = lax.broadcasted_iota(jnp.int32, (shapes, shapes), 0) == lax.broadcasted_iota(
            jnp.int32, (shapes, shapes), 1
        )
        column = jnp.sum(jnp.where(square, 0.5 * weight[0:1, :], 0.0), axis=1, keepdims=True)
        table[...] = jnp.broadcast_to(column, table.shape).astype(BF16)

    rows = out_ref.shape[0]
    first = place_ref[1] + pl.program_id(0) * rows
    position = first + lax.broadcasted_iota(jnp.int32, (rows, shapes), 0)
    inside = (position >= starts[0:1, :]) & (position < ends[0:1, :])
    out_ref[...] = dot(jnp.where(inside, 1.0, 0.0).astype(BF16), table[...]).astype(BF16)


def point_weights(place, shape_points, shape_category, category_counts, rows, average):
    shapes = shape_points.shape[0]
    padded = -(-shapes // LANES) * LANES
    wide = lambda v: jnp.broadcast_to(jnp.pad(v, (0, padded - shapes))[None, :], (8, padded))
    tile = pick_tile(rows)
    whole = pl.BlockSpec((8, padded), lambda i: (0, 0))
    return pl.pallas_call(
        functools.partial(point_weight_kernel, average),
        grid=(rows // tile,),
        in_specs=[
            pl.BlockSpec(memory_space=pltpu.SMEM),
            pl.BlockSpec(memory_space=pltpu.SMEM),
            whole,
            whole,
        ],
        out_specs=pl.BlockSpec((tile, LANES), lambda i: (i, 0)),
        out_shape=jax.ShapeDtypeStruct((rows, LANES), BF16),
        scratch_shapes=[pltpu.VMEM((padded, LANES), BF16)],
        compiler_params=pltpu.CompilerParams(vmem_limit_bytes=VMEM_BYTES),
        name="point_weight",
    )(place, category_counts, wide(shape_points), wide(shape_category))


def activate(half):
    one = jnp.asarray(1, BF16)
    half = half.astype(BF16)
    bent = jnp.tanh(half)
    lift = one + bent
    value = half * lift
    return value, lift + value * (one - bent)


def layers_kernel(masks, parts, *refs):
    gathered = refs[1:9]
    place_ref = refs[0]
    x_ref, cot_ref, pw_ref = refs[9:12]
    out_ref, in_grad_ref, keep_ref, send_ref = refs[12:16]
    dir_a, dir_b, w_a, w_b, wt_a, wt_b, gw_a, gw_b, vec, gsum = refs[16:26]
    step = pl.program_id(0)
    width = x_ref.shape[1]
    tile = x_ref.shape[0]
    sub = tile // parts

    def owner(slot):
        return place_ref[0] ^ masks[slot]

    @pl.when(step == 0)
    def _():
        lane = lax.broadcasted_iota(jnp.int32, (8, width), 1) // SLOT
        small = jnp.zeros((8, width), F32)
        for slot in range(len(masks)):
            home = owner(slot)
            rows = pl.ds(pl.multiple_of(home * SLOT, SLOT), SLOT)
            block = gathered[slot // 4][slot % 4]
            dir_a[rows, :] = block[:, 0:width]
            dir_b[rows, :] = block[:, width : 2 * width]
            extra = block[:, 2 * width :].astype(F32)[0:8]
            small = jnp.where(
                lane == home, jnp.concatenate([extra] * (width // LANES), axis=1), small
            )
        for k, (direction, w, wt) in enumerate(((dir_a, w_a, wt_a), (dir_b, w_b, wt_b))):
            full = direction[...].astype(F32)
            norm = lax.rsqrt(jnp.sum(full * full, axis=0, keepdims=True) + EPS)
            scale = small[2 * k : 2 * k + 1] * norm
            weight = (scale * full).astype(BF16)
            half = weight * jnp.asarray(0.5, BF16)
            w[...] = half
            wt[...] = (weight if k == 0 else half).T
            vec[3 * k : 3 * k + 1, :] = 0.5 * small[2 * k + 1 : 2 * k + 2]
            vec[3 * k + 1 : 3 * k + 2, :] = scale
            vec[3 * k + 2 : 3 * k + 3, :] = norm
        gw_a[...] = jnp.zeros_like(gw_a)
        gw_b[...] = jnp.zeros_like(gw_b)
        gsum[...] = jnp.zeros_like(gsum)

    spans = [pl.ds(k * sub, sub) for k in range(parts)]
    hidden, slope_a = zip(
        *[activate(dot(x_ref[s, :], w_a[...]) + vec[0:1, :]) for s in spans]
    )
    grads = []
    for s, h in zip(spans, hidden):
        value, slope_b = activate(dot(h, w_b[...]) + vec[3:4, :])
        out_ref[s, :] = value
        weight = jnp.concatenate([pw_ref[s, :]] * (width // LANES), axis=1)
        grads.append((cot_ref[s, :] * weight) * slope_b)
    grads_a = [dot(g, wt_b[...]).astype(BF16) * sa for g, sa in zip(grads, slope_a)]
    for s, g in zip(spans, grads_a):
        in_grad_ref[s, :] = dot(g, wt_a[...]).astype(BF16)
    ones = jnp.ones((SLOT, tile), BF16)
    join = lambda pieces: jnp.concatenate(pieces, axis=0)
    both = dot(join([join(hidden).T, ones]), join(grads))
    gw_b[...] += both[:width]
    gsum[8:16, :] += both[width : width + 8]
    both = dot(join([x_ref[...].T, ones]), join(grads_a))
    gw_a[...] += both[:width]
    gsum[0:8, :] += both[width : width + 8]

    @pl.when(step == pl.num_programs(0) - 1)
    def _():
        small = []
        for k, (direction, gw) in enumerate(((dir_a, gw_a), (dir_b, gw_b))):
            full = direction[...].astype(F32)
            grad = gw[...]
            scale, norm = vec[3 * k + 1 : 3 * k + 2, :], vec[3 * k + 2 : 3 * k + 3, :]
            inner = jnp.sum(grad * full, axis=0, keepdims=True)
            gw[...] = scale * grad - (scale * norm * norm * inner) * full
            small += [norm * inner, gsum[8 * k : 8 * k + 1, :]]
        gsum[0:8, :] = jnp.concatenate(small + [jnp.zeros((4, width), F32)], axis=0)
        for slot in range(len(masks)):
            home = owner(slot)
            rows = pl.ds(pl.multiple_of(home * SLOT, SLOT), SLOT)
            chunk = pl.ds(pl.multiple_of(home * SLOT // LANES * LANES, LANES), LANES)
            extra = pltpu.roll(gsum[0:8, chunk], LANES - home * SLOT % LANES, 1)
            extra = jnp.concatenate([extra, jnp.zeros((8, LANES), F32)], axis=0)
            block = jnp.concatenate([gw_a[rows, :], gw_b[rows, :], extra], axis=1)
            if slot < len(masks) // 2:
                keep_ref[slot] = block
            else:
                send_ref[slot - len(masks) // 2] = block.astype(BF16)


def layers(place, gathered, layer_input, cotangent, weights, masks):
    rows, width = layer_input.shape
    tile = pick_tile(rows)
    parts = 4 if tile % (4 * SLOT) == 0 else 1
    span = 2 * width + LANES
    half = len(masks) // 2
    by_row = lambda w: pl.BlockSpec((tile, w), lambda i: (i, 0))
    whole = lambda *dims: pl.BlockSpec(dims, lambda i: (0,) * len(dims))
    square = lambda dtype: pltpu.VMEM((width, width), dtype)
    return pl.pallas_call(
        functools.partial(layers_kernel, masks, parts),
        grid=(rows // tile,),
        in_specs=[pl.BlockSpec(memory_space=pltpu.SMEM)]
        + [whole(4, SLOT, span)] * 8
        + [by_row(width), by_row(width), by_row(LANES)],
        out_specs=[by_row(width), by_row(width), whole(half, SLOT, span), whole(half, SLOT, span)],
        out_shape=[
            jax.ShapeDtypeStruct((rows, width), BF16),
            jax.ShapeDtypeStruct((rows, width), BF16),
            jax.ShapeDtypeStruct((half, SLOT, span), F32),
            jax.ShapeDtypeStruct((half, SLOT, span), BF16),
        ],
        scratch_shapes=[square(BF16)] * 6
        + [square(F32)] * 2
        + [pltpu.VMEM((8, width), F32), pltpu.VMEM((16, width), F32)],
        compiler_params=pltpu.CompilerParams(vmem_limit_bytes=VMEM_BYTES),
        name="layers",
    )(place, *gathered, layer_input, cotangent, weights)


def swap(value, mask, groups):
    return lax.ppermute(value, AXES, [(k, k ^ mask) for k in range(groups)])


def body(
    layer_input,
    cotangent,
    shape_points,
    shape_category,
    category_counts,
    dir_a,
    gain_a,
    bias_a,
    dir_b,
    gain_b,
    bias_b,
):
    dp, fsdp = lax.axis_size("dp"), lax.axis_size("fsdp")
    groups = dp * fsdp
    rows, width = layer_input.shape
    share = dir_a.shape[0]
    slots = width // SLOT
    average = groups * rows // shape_points.shape[0]
    me = lax.axis_index(AXES).astype(jnp.int32)
    fast = share == SLOT and groups == 32 and fsdp == 8
    small = jnp.stack([gain_a, bias_a, gain_b, bias_b])
    place = jnp.stack([me if fast else jnp.zeros_like(me), me * rows])
    if fast:
        extra = jnp.pad(jnp.tile(small, (1, LANES // SLOT)), ((0, SLOT - 4), (0, 0)))
        mine = jnp.concatenate([dir_a, dir_b, extra], axis=1)[None]
        near = [mine] + [swap(mine, m, groups) for m in (2, 4, 6)]
        near = jnp.concatenate(near, axis=0)
        wide = [near] + [swap(near, m, groups) for m in (1, 16, 17)]
        gathered = wide + [swap(v, 8, groups) for v in wide]
        masks = [c ^ xy ^ z for c in (0, 8) for xy in (0, 1, 16, 17) for z in (0, 2, 4, 6)]
    else:
        full = [lax.all_gather(v, AXES, axis=0, tiled=True) for v in (dir_a, dir_b)]
        vectors = lax.all_gather(small, AXES, axis=1, tiled=True)
        extra = jnp.tile(vectors.reshape(4, slots, SLOT).transpose(1, 0, 2), (1, 1, LANES // SLOT))
        extra = jnp.pad(extra, ((0, 0), (0, SLOT - 4), (0, 0)))
        blocks = [v.reshape(slots, SLOT, width) for v in full] + [extra]
        blocks = jnp.concatenate(blocks, axis=2)
        gathered = [blocks[4 * k : 4 * k + 4] for k in range(8)]
        masks = list(range(slots))
    weights = point_weights(place, shape_points, shape_category, category_counts, rows, average)
    layer_output, input_grad, keep, send = layers(
        place, gathered, layer_input, cotangent, weights, masks
    )
    if fast:
        total = keep + swap(send, 8, groups).astype(F32)
        parts = [total[4 * k : 4 * k + 4] for k in range(4)]
        came = [swap(parts[k].astype(BF16), m, groups) for k, m in ((1, 1), (2, 16), (3, 17))]
        total = parts[0] + sum(v.astype(F32) for v in came)
        came = [swap(total[k].astype(BF16), m, groups) for k, m in ((1, 2), (2, 4), (3, 6))]
        total = total[0] + sum(v.astype(F32) for v in came)
        vectors = total[0:4, 2 * width : 2 * width + SLOT]
        grad_a, grad_b = total[:, :width], total[:, width : 2 * width]
    else:
        total = jnp.concatenate([keep, send.astype(F32)], axis=0)
        scatter = lambda v, d: lax.psum_scatter(v, AXES, scatter_dimension=d, tiled=True)
        square = total[:, :, : 2 * width].reshape(width, 2 * width)
        square = scatter(square, 0)
        grad_a, grad_b = square[:, :width], square[:, width:]
        vectors = total[:, 0:4, 2 * width : 2 * width + SLOT].transpose(1, 0, 2).reshape(4, width)
        vectors = scatter(vectors, 1)
    return (
        layer_output,
        input_grad,
        grad_a,
        vectors[0],
        vectors[1],
        grad_b,
        vectors[2],
        vectors[3],
    )


def solution(mesh):
    rows, row, none = P(AXES, None), P(AXES), P()
    in_specs = (rows, rows, none, none, none, rows, row, row, rows, row, row)
    out_specs = (rows, rows, rows, row, row, rows, row, row)
    return jax.shard_map(body, mesh=mesh, in_specs=in_specs, out_specs=out_specs, check_vma=False)
```

```python
import functools
import math

import jax
import jax.numpy as jnp
from jax import lax
from jax.experimental import pallas as pl
from jax.experimental.pallas import tpu as pltpu
from jax.sharding import PartitionSpec as P

AXES = ("dp", "fsdp")
EPS = 1e-06
SLOT = 16
LANES = 128
F32 = jnp.float32
BF16 = jnp.bfloat16
VMEM_BYTES = 44 << 20


def pick_tile(rows):
    for tile in (1472, 736, 512, 368, 256, 128, 64, 32, 16):
        if rows % tile == 0:
            return tile
    return rows


def dot(left, right):
    return jnp.dot(left, right, preferred_element_type=F32)


def point_weight_kernel(average, place_ref, counts_ref, points_ref, category_ref, mine_ref, out_ref, same_ref, table):
    lines = out_ref.shape[0] // LANES
    step = pl.program_id(0)

    @pl.when(step == 0)
    def _():
        same_ref[...] = mine_ref[...]
        line = lax.broadcasted_iota(jnp.int32, table.shape, 0)
        position = place_ref[1] + line * LANES + lax.broadcasted_iota(jnp.int32, table.shape, 1)

        def enter(shape, carry):
            start, count, points = carry
            after = position >= start
            count = jnp.where(after, counts_ref[category_ref[shape]], count)
            points = jnp.where(after, points_ref[shape], points)
            return start + points_ref[shape], count, points

        zero = jnp.zeros(table.shape, jnp.int32)
        shapes = points_ref.shape[0]
        _, count, points = lax.fori_loop(
            0, shapes, enter, (jnp.int32(0), zero, zero), unroll=math.gcd(shapes, 8)
        )
        table[...] = (
            count.astype(F32)
            * (average / 8.0)
            / jnp.maximum(points, average // 2).astype(F32)
        )

    for k in range(lines):
        row = jnp.broadcast_to(table[pl.ds(step * lines + k, 1), :], (LANES, LANES))
        out_ref[pl.ds(k * LANES, LANES), :] = row.T.astype(BF16)


def point_weights(place, shape_points, shape_category, category_counts, mine, rows, average):
    scalars = pl.BlockSpec(memory_space=pltpu.SMEM)
    steps = 4 if rows % (4 * LANES) == 0 else 1
    lines = -(-rows // LANES // 8) * 8
    whole = pl.BlockSpec(mine.shape, lambda i: (0,) * mine.ndim)
    return pl.pallas_call(
        functools.partial(point_weight_kernel, average),
        grid=(steps,),
        in_specs=[scalars] * 4 + [whole],
        out_specs=[pl.BlockSpec((rows // steps, LANES), lambda i: (i, 0)), whole],
        out_shape=[
            jax.ShapeDtypeStruct((rows, LANES), BF16),
            jax.ShapeDtypeStruct(mine.shape, mine.dtype),
        ],
        scratch_shapes=[pltpu.VMEM((lines, LANES), F32)],
        compiler_params=pltpu.CompilerParams(vmem_limit_bytes=16 << 20),
        cost_estimate=pl.CostEstimate(
            flops=50 * rows * LANES, bytes_accessed=2 * rows * LANES, transcendentals=0
        ),
        name="point_weight",
    )(place, category_counts, shape_points, shape_category, mine)


def activate(half):
    lift = 1.0 + jnp.tanh(half)
    value = (half * lift).astype(BF16)
    lift = lift.astype(BF16)
    return value, lift + value * (jnp.asarray(2, BF16) - lift)


def layers_kernel(masks, parts, *refs):
    gathered = refs[1:9]
    place_ref = refs[0]
    x_ref, cot_ref, pw_ref = refs[9:12]
    out_ref, in_grad_ref, keep_ref, send_ref = refs[12:16]
    dir_a, dir_b, w_a, w_b, wt_a, wt_b, gw_a, gw_b, vec, gsum, landed, columns, arrived = refs[16:]
    step = pl.program_id(0)
    width = x_ref.shape[1]
    tile = x_ref.shape[0]
    sub = tile // parts

    def owner(slot):
        return place_ref[0] ^ masks[slot]

    @pl.when(step == 0)
    def _():
        copies = [
            pltpu.make_async_copy(ref, landed.at[k], arrived.at[k])
            for k, ref in enumerate(gathered)
        ]
        for copy in copies:
            copy.start()
        for copy in copies:
            copy.wait()
        for slot in range(len(masks)):
            rows = pl.ds(pl.multiple_of(owner(slot) * SLOT, SLOT), SLOT)
            block = landed[slot // 4, slot % 4]
            dir_a[rows, :] = block[:, 0:width]
            dir_b[rows, :] = block[:, width : 2 * width]
            columns[rows, :] = block[:, 2 * width :].astype(F32)
        small = columns[...].T
        for k, (direction, w, wt) in enumerate(((dir_a, w_a, wt_a), (dir_b, w_b, wt_b))):
            full = direction[...].astype(F32)
            norm = lax.rsqrt(jnp.sum(full * full, axis=0, keepdims=True) + EPS)
            scale = small[2 * k : 2 * k + 1] * norm
            weight = (scale * full).astype(BF16)
            half = weight * jnp.asarray(0.5, BF16)
            w[...] = half
            wt[...] = (weight if k == 0 else half).T
            vec[3 * k : 3 * k + 1, :] = 0.5 * small[2 * k + 1 : 2 * k + 2]
            vec[3 * k + 1 : 3 * k + 2, :] = scale
            vec[3 * k + 2 : 3 * k + 3, :] = norm
        gw_a[...] = jnp.zeros_like(gw_a)
        gw_b[...] = jnp.zeros_like(gw_b)
        gsum[...] = jnp.zeros_like(gsum)

    spans = [pl.ds(k * sub, sub) for k in range(parts)]
    hidden, slope_a = zip(
        *[activate(dot(x_ref[s, :], w_a[...]) + vec[0:1, :]) for s in spans]
    )
    grads = []
    for s, h in zip(spans, hidden):
        value, slope_b = activate(dot(h, w_b[...]) + vec[3:4, :])
        out_ref[s, :] = value
        weight = jnp.concatenate([pw_ref[s, :]] * (width // LANES), axis=1)
        grads.append((cot_ref[s, :] * weight) * slope_b)
    grads_a = [dot(g, wt_b[...]).astype(BF16) * sa for g, sa in zip(grads, slope_a)]
    for s, g in zip(spans, grads_a):
        in_grad_ref[s, :] = dot(g, wt_a[...]).astype(BF16)
    ones = jnp.ones((SLOT, tile), BF16)
    join = lambda pieces: jnp.concatenate(pieces, axis=0)
    both = dot(join([join(hidden).T, ones]), join(grads))
    gw_b[...] += both[:width]
    gsum[8:16, :] += both[width : width + 8]
    both = dot(join([x_ref[...].T, ones]), join(grads_a))
    gw_a[...] += both[:width]
    gsum[0:8, :] += both[width : width + 8]

    @pl.when(step == pl.num_programs(0) - 1)
    def _():
        small = []
        for k, (direction, gw) in enumerate(((dir_a, gw_a), (dir_b, gw_b))):
            full = direction[...].astype(F32)
            grad = gw[...]
            scale, norm = vec[3 * k + 1 : 3 * k + 2, :], vec[3 * k + 2 : 3 * k + 3, :]
            inner = jnp.sum(grad * full, axis=0, keepdims=True)
            gw[...] = scale * grad - (scale * norm * norm * inner) * full
            small += [norm * inner, gsum[8 * k : 8 * k + 1, :]]
        gsum[0:8, :] = jnp.concatenate(small + [jnp.zeros((4, width), F32)], axis=0)
        for slot in range(len(masks)):
            home = owner(slot)
            rows = pl.ds(pl.multiple_of(home * SLOT, SLOT), SLOT)
            chunk = pl.ds(pl.multiple_of(home * SLOT // LANES * LANES, LANES), LANES)
            extra = pltpu.roll(gsum[0:8, chunk], LANES - home * SLOT % LANES, 1)
            extra = jnp.concatenate([extra, jnp.zeros((8, LANES), F32)], axis=0)
            block = jnp.concatenate([gw_a[rows, :], gw_b[rows, :], extra], axis=1)
            if slot < len(masks) // 2:
                keep_ref[slot] = block
            else:
                send_ref[slot - len(masks) // 2] = block.astype(BF16)


def layers(place, gathered, layer_input, cotangent, weights, masks):
    rows, width = layer_input.shape
    tile = pick_tile(rows)
    parts = 4 if tile % (4 * SLOT) == 0 else 1
    span = 2 * width + LANES
    half = len(masks) // 2
    by_row = lambda w: pl.BlockSpec((tile, w), lambda i: (i, 0))
    whole = lambda *dims: pl.BlockSpec(dims, lambda i: (0,) * len(dims))
    square = lambda dtype: pltpu.VMEM((width, width), dtype)
    return pl.pallas_call(
        functools.partial(layers_kernel, masks, parts),
        grid=(rows // tile,),
        in_specs=[pl.BlockSpec(memory_space=pltpu.SMEM)]
        + [pl.BlockSpec(memory_space=pl.ANY)] * 8
        + [by_row(width), by_row(width), by_row(LANES)],
        out_specs=[by_row(width), by_row(width), whole(half, SLOT, span), whole(half, SLOT, span)],
        out_shape=[
            jax.ShapeDtypeStruct((rows, width), BF16),
            jax.ShapeDtypeStruct((rows, width), BF16),
            jax.ShapeDtypeStruct((half, SLOT, span), F32),
            jax.ShapeDtypeStruct((half, SLOT, span), BF16),
        ],
        scratch_shapes=[square(BF16)] * 6
        + [square(F32)] * 2
        + [
            pltpu.VMEM((8, width), F32),
            pltpu.VMEM((16, width), F32),
            pltpu.VMEM((8, 4, SLOT, span), BF16),
            pltpu.VMEM((width, LANES), F32),
            pltpu.SemaphoreType.DMA((8,)),
        ],
        compiler_params=pltpu.CompilerParams(vmem_limit_bytes=VMEM_BYTES),
        name="layers",
    )(place, *gathered, layer_input, cotangent, weights)


def swap(value, mask, groups):
    return lax.ppermute(value, AXES, [(k, k ^ mask) for k in range(groups)])


def body(
    layer_input,
    cotangent,
    shape_points,
    shape_category,
    category_counts,
    dir_a,
    gain_a,
    bias_a,
    dir_b,
    gain_b,
    bias_b,
):
    dp, fsdp = lax.axis_size("dp"), lax.axis_size("fsdp")
    groups = dp * fsdp
    rows, width = layer_input.shape
    share = dir_a.shape[0]
    slots = width // SLOT
    average = groups * rows // shape_points.shape[0]
    me = lax.axis_index(AXES).astype(jnp.int32)
    fast = share == SLOT and groups == 32 and fsdp == 8
    small = jnp.stack([gain_a, bias_a, gain_b, bias_b])
    place = jnp.stack([me if fast else jnp.zeros_like(me), me * rows])
    weigh = lambda held: point_weights(
        place, shape_points, shape_category, category_counts, held, rows, average
    )
    if fast:
        extra = jnp.pad(small.T, ((0, 0), (0, LANES - 4)))
        mine = jnp.concatenate([dir_a, dir_b, extra], axis=1)[None]
        weights, same = weigh(mine)
        near = [same] + [swap(mine, m, groups) for m in (2, 4, 6)]
        near = jnp.concatenate(near, axis=0)
        wide = [near] + [swap(near, m, groups) for m in (1, 16, 17)]
        gathered = wide + [swap(v, 8, groups) for v in wide]
        masks = [c ^ xy ^ z for c in (0, 8) for xy in (0, 1, 16, 17) for z in (0, 2, 4, 6)]
    else:
        full = [lax.all_gather(v, AXES, axis=0, tiled=True) for v in (dir_a, dir_b)]
        vectors = lax.all_gather(small, AXES, axis=1, tiled=True)
        extra = jnp.pad(vectors.T.reshape(slots, SLOT, 4), ((0, 0), (0, 0), (0, LANES - 4)))
        blocks = [v.reshape(slots, SLOT, width) for v in full] + [extra]
        blocks = jnp.concatenate(blocks, axis=2)
        gathered = [blocks[4 * k : 4 * k + 4] for k in range(8)]
        masks = list(range(slots))
        weights, _ = weigh(dir_a)
    layer_output, input_grad, keep, send = layers(
        place, gathered, layer_input, cotangent, weights, masks
    )
    if fast:
        total = keep + swap(send, 8, groups).astype(F32)
        parts = [total[4 * k : 4 * k + 4] for k in range(4)]
        came = [swap(parts[k].astype(BF16), m, groups) for k, m in ((1, 1), (2, 16), (3, 17))]
        total = parts[0] + sum(v.astype(F32) for v in came)
        came = [swap(total[k].astype(BF16), m, groups) for k, m in ((1, 2), (2, 4), (3, 6))]
        total = total[0] + sum(v.astype(F32) for v in came)
        vectors = total[0:4, 2 * width : 2 * width + SLOT]
        grad_a, grad_b = total[:, :width], total[:, width : 2 * width]
    else:
        total = jnp.concatenate([keep, send.astype(F32)], axis=0)
        scatter = lambda v, d: lax.psum_scatter(v, AXES, scatter_dimension=d, tiled=True)
        square = total[:, :, : 2 * width].reshape(width, 2 * width)
        square = scatter(square, 0)
        grad_a, grad_b = square[:, :width], square[:, width:]
        vectors = total[:, 0:4, 2 * width : 2 * width + SLOT].transpose(1, 0, 2).reshape(4, width)
        vectors = scatter(vectors, 1)
    return (
        layer_output,
        input_grad,
        grad_a,
        vectors[0],
        vectors[1],
        grad_b,
        vectors[2],
        vectors[3],
    )


def solution(mesh):
    rows, row, none = P(AXES, None), P(AXES), P()
    in_specs = (rows, rows, none, none, none, rows, row, row, rows, row, row)
    out_specs = (rows, rows, rows, row, row, rows, row, row)
    return jax.shard_map(body, mesh=mesh, in_specs=in_specs, out_specs=out_specs, check_vma=False)
```

```python
import functools
import math

import jax
import jax.numpy as jnp
from jax import lax
from jax.experimental import pallas as pl
from jax.experimental.pallas import tpu as pltpu
from jax.sharding import PartitionSpec as P

AXES = ("dp", "fsdp")
EPS = 1e-06
SLOT = 16
LANES = 128
F32 = jnp.float32
BF16 = jnp.bfloat16
VMEM_BYTES = 36 << 20
GRAD_VMEM = 10 << 20


def pick_tile(rows):
    for tile in (1472, 736, 512, 368, 256, 128, 64, 32, 16):
        if rows % tile == 0:
            return tile
    return rows


def dot(left, right):
    return jnp.dot(left, right, preferred_element_type=F32)


def point_weight_kernel(average, place_ref, counts_ref, points_ref, category_ref, mine_ref, out_ref, same_ref, table):
    lines = out_ref.shape[0] // LANES
    step = pl.program_id(0)

    @pl.when(step == 0)
    def _():
        same_ref[...] = mine_ref[...]
        line = lax.broadcasted_iota(jnp.int32, table.shape, 0)
        position = place_ref[1] + line * LANES + lax.broadcasted_iota(jnp.int32, table.shape, 1)

        def enter(shape, carry):
            start, count, points = carry
            after = position >= start
            count = jnp.where(after, counts_ref[category_ref[shape]], count)
            points = jnp.where(after, points_ref[shape], points)
            return start + points_ref[shape], count, points

        zero = jnp.zeros(table.shape, jnp.int32)
        shapes = points_ref.shape[0]
        _, count, points = lax.fori_loop(
            0, shapes, enter, (jnp.int32(0), zero, zero), unroll=math.gcd(shapes, 8)
        )
        table[...] = (
            count.astype(F32)
            * (average / 8.0)
            / jnp.maximum(points, average // 2).astype(F32)
        )

    for k in range(lines):
        row = jnp.broadcast_to(table[pl.ds(step * lines + k, 1), :], (LANES, LANES))
        out_ref[pl.ds(k * LANES, LANES), :] = row.T.astype(BF16)


def point_weights(place, shape_points, shape_category, category_counts, mine, rows, average):
    scalars = pl.BlockSpec(memory_space=pltpu.SMEM)
    steps = 4 if rows % (4 * LANES) == 0 else 1
    lines = -(-rows // LANES // 8) * 8
    whole = pl.BlockSpec(mine.shape, lambda i: (0,) * mine.ndim)
    return pl.pallas_call(
        functools.partial(point_weight_kernel, average),
        grid=(steps,),
        in_specs=[scalars] * 4 + [whole],
        out_specs=[pl.BlockSpec((rows // steps, LANES), lambda i: (i, 0)), whole],
        out_shape=[
            jax.ShapeDtypeStruct((rows, LANES), BF16),
            jax.ShapeDtypeStruct(mine.shape, mine.dtype),
        ],
        scratch_shapes=[pltpu.VMEM((lines, LANES), F32)],
        compiler_params=pltpu.CompilerParams(vmem_limit_bytes=16 << 20),
        cost_estimate=pl.CostEstimate(
            flops=50 * rows * LANES, bytes_accessed=2 * rows * LANES, transcendentals=0
        ),
        name="point_weight",
    )(place, category_counts, shape_points, shape_category, mine)


def input_grad_kernel(grad_ref, w_ref, held_ref, *refs):
    out_ref, same_ref = refs[-2:]

    @pl.when(pl.program_id(0) == 0)
    def _():
        same_ref[...] = held_ref[...]

    out_ref[...] = dot(grad_ref[...], w_ref[...]).astype(BF16)


def input_grads(grads, weight, held, whole, tile, first, count):
    rows, width = grads.shape
    by_row = pl.BlockSpec((tile, width), lambda i: (i + first, 0))
    every = pl.BlockSpec(held.shape, lambda i: (0,) * held.ndim)
    more = [] if whole is None else [whole]
    return pl.pallas_call(
        input_grad_kernel,
        grid=(count,),
        in_specs=[by_row, pl.BlockSpec((width, width), lambda i: (0, 0)), every]
        + [pl.BlockSpec(memory_space=pl.ANY)] * len(more),
        out_specs=[by_row, every],
        out_shape=[
            jax.ShapeDtypeStruct((rows, width), BF16),
            jax.ShapeDtypeStruct(held.shape, held.dtype),
        ],
        input_output_aliases={3: 0} if more else {},
        cost_estimate=pl.CostEstimate(
            flops=2 * count * tile * width * width,
            bytes_accessed=4 * count * tile * width,
            transcendentals=0,
        ),
        compiler_params=pltpu.CompilerParams(vmem_limit_bytes=GRAD_VMEM),
        name="input_grad",
    )(grads, weight, held, *more)


def activate(half):
    lift = 1.0 + jnp.tanh(half)
    value = (half * lift).astype(BF16)
    lift = lift.astype(BF16)
    return value, lift + value * (jnp.asarray(2, BF16) - lift)


def layers_kernel(masks, parts, *refs):
    gathered = refs[1:9]
    place_ref = refs[0]
    x_ref, cot_ref, pw_ref = refs[9:12]
    out_ref, grad_ref, wt_a, keep_ref, send_ref = refs[12:17]
    dir_a, dir_b, w_a, w_b, wt_b, gw_a, gw_b, vec, gsum, landed, columns, arrived = refs[17:]
    step = pl.program_id(0)
    width = x_ref.shape[1]
    tile = x_ref.shape[0]
    sub = tile // parts

    def owner(slot):
        return place_ref[0] ^ masks[slot]

    @pl.when(step == 0)
    def _():
        copies = [
            pltpu.make_async_copy(ref, landed.at[k], arrived.at[k])
            for k, ref in enumerate(gathered)
        ]
        for copy in copies:
            copy.start()
        for copy in copies:
            copy.wait()
        for slot in range(len(masks)):
            rows = pl.ds(pl.multiple_of(owner(slot) * SLOT, SLOT), SLOT)
            block = landed[slot // 4, slot % 4]
            dir_a[rows, :] = block[:, 0:width]
            dir_b[rows, :] = block[:, width : 2 * width]
            columns[rows, :] = block[:, 2 * width :].astype(F32)
        small = columns[...].T
        for k, (direction, w, wt) in enumerate(((dir_a, w_a, wt_a), (dir_b, w_b, wt_b))):
            full = direction[...].astype(F32)
            norm = lax.rsqrt(jnp.sum(full * full, axis=0, keepdims=True) + EPS)
            scale = small[2 * k : 2 * k + 1] * norm
            weight = (scale * full).astype(BF16)
            half = weight * jnp.asarray(0.5, BF16)
            w[...] = half
            wt[...] = (weight if k == 0 else half).T
            vec[3 * k : 3 * k + 1, :] = 0.5 * small[2 * k + 1 : 2 * k + 2]
            vec[3 * k + 1 : 3 * k + 2, :] = scale
            vec[3 * k + 2 : 3 * k + 3, :] = norm
        gw_a[...] = jnp.zeros_like(gw_a)
        gw_b[...] = jnp.zeros_like(gw_b)
        gsum[...] = jnp.zeros_like(gsum)

    spans = [pl.ds(k * sub, sub) for k in range(parts)]
    hidden, slope_a = zip(
        *[activate(dot(x_ref[s, :], w_a[...]) + vec[0:1, :]) for s in spans]
    )
    grads = []
    for s, h in zip(spans, hidden):
        value, slope_b = activate(dot(h, w_b[...]) + vec[3:4, :])
        out_ref[s, :] = value
        weight = jnp.concatenate([pw_ref[s, :]] * (width // LANES), axis=1)
        grads.append((cot_ref[s, :] * weight) * slope_b)
    grads_a = [dot(g, wt_b[...]).astype(BF16) * sa for g, sa in zip(grads, slope_a)]
    for s, g in zip(spans, grads_a):
        grad_ref[s, :] = g
    ones = jnp.ones((SLOT, tile), BF16)
    join = lambda pieces: jnp.concatenate(pieces, axis=0)
    both = dot(join([join(hidden).T, ones]), join(grads))
    gw_b[...] += both[:width]
    gsum[8:16, :] += both[width : width + 8]
    both = dot(join([x_ref[...].T, ones]), join(grads_a))
    gw_a[...] += both[:width]
    gsum[0:8, :] += both[width : width + 8]

    @pl.when(step == pl.num_programs(0) - 1)
    def _():
        small = []
        for k, (direction, gw) in enumerate(((dir_a, gw_a), (dir_b, gw_b))):
            full = direction[...].astype(F32)
            grad = gw[...]
            scale, norm = vec[3 * k + 1 : 3 * k + 2, :], vec[3 * k + 2 : 3 * k + 3, :]
            inner = jnp.sum(grad * full, axis=0, keepdims=True)
            gw[...] = scale * grad - (scale * norm * norm * inner) * full
            small += [norm * inner, gsum[8 * k : 8 * k + 1, :]]
        gsum[0:8, :] = jnp.concatenate(small + [jnp.zeros((4, width), F32)], axis=0)
        for slot in range(len(masks)):
            home = owner(slot)
            rows = pl.ds(pl.multiple_of(home * SLOT, SLOT), SLOT)
            chunk = pl.ds(pl.multiple_of(home * SLOT // LANES * LANES, LANES), LANES)
            extra = pltpu.roll(gsum[0:8, chunk], LANES - home * SLOT % LANES, 1)
            extra = jnp.concatenate([extra, jnp.zeros((8, LANES), F32)], axis=0)
            block = jnp.concatenate([gw_a[rows, :], gw_b[rows, :], extra], axis=1)
            if slot < len(masks) // 2:
                keep_ref[slot] = block
            else:
                send_ref[slot - len(masks) // 2] = block.astype(BF16)


def layers(place, gathered, layer_input, cotangent, weights, masks):
    rows, width = layer_input.shape
    tile = pick_tile(rows)
    parts = 4 if tile % (4 * SLOT) == 0 else 1
    span = 2 * width + LANES
    half = len(masks) // 2
    by_row = lambda w: pl.BlockSpec((tile, w), lambda i: (i, 0))
    whole = lambda *dims: pl.BlockSpec(dims, lambda i: (0,) * len(dims))
    square = lambda dtype: pltpu.VMEM((width, width), dtype)
    return pl.pallas_call(
        functools.partial(layers_kernel, masks, parts),
        grid=(rows // tile,),
        in_specs=[pl.BlockSpec(memory_space=pltpu.SMEM)]
        + [pl.BlockSpec(memory_space=pl.ANY)] * 8
        + [by_row(width), by_row(width), by_row(LANES)],
        out_specs=[
            by_row(width),
            by_row(width),
            whole(width, width),
            whole(half, SLOT, span),
            whole(half, SLOT, span),
        ],
        out_shape=[
            jax.ShapeDtypeStruct((rows, width), BF16),
            pltpu.VMEM((rows, width), BF16),
            jax.ShapeDtypeStruct((width, width), BF16),
            jax.ShapeDtypeStruct((half, SLOT, span), F32),
            jax.ShapeDtypeStruct((half, SLOT, span), BF16),
        ],
        scratch_shapes=[square(BF16)] * 5
        + [square(F32)] * 2
        + [
            pltpu.VMEM((8, width), F32),
            pltpu.VMEM((16, width), F32),
            pltpu.VMEM((8, 4, SLOT, span), BF16),
            pltpu.VMEM((width, LANES), F32),
            pltpu.SemaphoreType.DMA((8,)),
        ],
        compiler_params=pltpu.CompilerParams(vmem_limit_bytes=VMEM_BYTES),
        name="layers",
    )(place, *gathered, layer_input, cotangent, weights)


def swap(value, mask, groups):
    return lax.ppermute(value, AXES, [(k, k ^ mask) for k in range(groups)])


def body(
    layer_input,
    cotangent,
    shape_points,
    shape_category,
    category_counts,
    dir_a,
    gain_a,
    bias_a,
    dir_b,
    gain_b,
    bias_b,
):
    dp, fsdp = lax.axis_size("dp"), lax.axis_size("fsdp")
    groups = dp * fsdp
    rows, width = layer_input.shape
    share = dir_a.shape[0]
    slots = width // SLOT
    average = groups * rows // shape_points.shape[0]
    me = lax.axis_index(AXES).astype(jnp.int32)
    fast = share == SLOT and groups == 32 and fsdp == 8
    small = jnp.stack([gain_a, bias_a, gain_b, bias_b])
    place = jnp.stack([me if fast else jnp.zeros_like(me), me * rows])
    weigh = lambda held: point_weights(
        place, shape_points, shape_category, category_counts, held, rows, average
    )
    if fast:
        extra = jnp.pad(small.T, ((0, 0), (0, LANES - 4)))
        mine = jnp.concatenate([dir_a, dir_b, extra], axis=1)[None]
        weights, same = weigh(mine)
        near = [same] + [swap(mine, m, groups) for m in (2, 4, 6)]
        near = jnp.concatenate(near, axis=0)
        wide = [near] + [swap(near, m, groups) for m in (1, 16, 17)]
        gathered = wide + [swap(v, 8, groups) for v in wide]
        masks = [c ^ xy ^ z for c in (0, 8) for xy in (0, 1, 16, 17) for z in (0, 2, 4, 6)]
    else:
        full = [lax.all_gather(v, AXES, axis=0, tiled=True) for v in (dir_a, dir_b)]
        vectors = lax.all_gather(small, AXES, axis=1, tiled=True)
        extra = jnp.pad(vectors.T.reshape(slots, SLOT, 4), ((0, 0), (0, 0), (0, LANES - 4)))
        blocks = [v.reshape(slots, SLOT, width) for v in full] + [extra]
        blocks = jnp.concatenate(blocks, axis=2)
        gathered = [blocks[4 * k : 4 * k + 4] for k in range(8)]
        masks = list(range(slots))
        weights, _ = weigh(dir_a)
    tile = pick_tile(rows)
    tiles = rows // tile
    first = tiles * 5 // 8
    layer_output, grads, weight, keep, send = layers(
        place, gathered, layer_input, cotangent, weights, masks
    )
    if fast:
        total = keep + swap(send, 8, groups).astype(F32)
        parts = [total[4 * k : 4 * k + 4] for k in range(4)]
        came = [swap(parts[k].astype(BF16), m, groups) for k, m in ((1, 1), (2, 16), (3, 17))]
        input_grad, held = input_grads(grads, weight, parts[0], None, tile, 0, first)
        total = held + sum(v.astype(F32) for v in came)
        came = [swap(total[k].astype(BF16), m, groups) for k, m in ((1, 2), (2, 4), (3, 6))]
        input_grad, held = input_grads(
            grads, weight, total[0], input_grad, tile, first, tiles - first
        )
        total = held + sum(v.astype(F32) for v in came)
        vectors = total[0:4, 2 * width : 2 * width + SLOT]
        grad_a, grad_b = total[:, :width], total[:, width : 2 * width]
    else:
        input_grad, _ = input_grads(grads, weight, keep[0], None, tile, 0, tiles)
        total = jnp.concatenate([keep, send.astype(F32)], axis=0)
        scatter = lambda v, d: lax.psum_scatter(v, AXES, scatter_dimension=d, tiled=True)
        square = total[:, :, : 2 * width].reshape(width, 2 * width)
        square = scatter(square, 0)
        grad_a, grad_b = square[:, :width], square[:, width:]
        vectors = total[:, 0:4, 2 * width : 2 * width + SLOT].transpose(1, 0, 2).reshape(4, width)
        vectors = scatter(vectors, 1)
    return (
        layer_output,
        input_grad,
        grad_a,
        vectors[0],
        vectors[1],
        grad_b,
        vectors[2],
        vectors[3],
    )


def solution(mesh):
    rows, row, none = P(AXES, None), P(AXES), P()
    in_specs = (rows, rows, none, none, none, rows, row, row, rows, row, row)
    out_specs = (rows, rows, rows, row, row, rows, row, row)
    return jax.shard_map(body, mesh=mesh, in_specs=in_specs, out_specs=out_specs, check_vma=False)
```

```python
import functools
import math

import jax
import jax.numpy as jnp
from jax import lax
from jax.experimental import pallas as pl
from jax.experimental.pallas import tpu as pltpu
from jax.sharding import PartitionSpec as P

AXES = ("dp", "fsdp")
EPS = 1e-06
SLOT = 16
LANES = 128
F32 = jnp.float32
BF16 = jnp.bfloat16
VMEM_BYTES = 36 << 20
GRAD_VMEM = 10 << 20


def pick_tile(rows):
    for tile in (1472, 736, 512, 368, 256, 128, 64, 32, 16):
        if rows % tile == 0:
            return tile
    return rows


def dot(left, right):
    return jnp.dot(left, right, preferred_element_type=F32)


def point_weight_kernel(average, place_ref, counts_ref, points_ref, category_ref, mine_ref, out_ref, same_ref, table):
    lines = out_ref.shape[0] // LANES
    step = pl.program_id(0)

    @pl.when(step == 0)
    def _():
        same_ref[...] = mine_ref[...]
        line = lax.broadcasted_iota(jnp.int32, table.shape, 0)
        position = place_ref[1] + line * LANES + lax.broadcasted_iota(jnp.int32, table.shape, 1)

        def enter(shape, carry):
            start, count, points = carry
            after = position >= start
            count = jnp.where(after, counts_ref[category_ref[shape]], count)
            points = jnp.where(after, points_ref[shape], points)
            return start + points_ref[shape], count, points

        zero = jnp.zeros(table.shape, jnp.int32)
        shapes = points_ref.shape[0]
        _, count, points = lax.fori_loop(
            0, shapes, enter, (jnp.int32(0), zero, zero), unroll=math.gcd(shapes, 8)
        )
        table[...] = (
            count.astype(F32)
            * (average / 8.0)
            / jnp.maximum(points, average // 2).astype(F32)
        )

    for k in range(lines):
        row = jnp.broadcast_to(table[pl.ds(step * lines + k, 1), :], (LANES, LANES))
        out_ref[pl.ds(k * LANES, LANES), :] = row.T.astype(BF16)


def point_weights(place, shape_points, shape_category, category_counts, mine, rows, average):
    scalars = pl.BlockSpec(memory_space=pltpu.SMEM)
    steps = 4 if rows % (4 * LANES) == 0 else 1
    lines = -(-rows // LANES // 8) * 8
    whole = pl.BlockSpec(mine.shape, lambda i: (0,) * mine.ndim)
    return pl.pallas_call(
        functools.partial(point_weight_kernel, average),
        grid=(steps,),
        in_specs=[scalars] * 4 + [whole],
        out_specs=[pl.BlockSpec((rows // steps, LANES), lambda i: (i, 0)), whole],
        out_shape=[
            jax.ShapeDtypeStruct((rows, LANES), BF16),
            jax.ShapeDtypeStruct(mine.shape, mine.dtype),
        ],
        scratch_shapes=[pltpu.VMEM((lines, LANES), F32)],
        compiler_params=pltpu.CompilerParams(vmem_limit_bytes=16 << 20),
        cost_estimate=pl.CostEstimate(
            flops=50 * rows * LANES, bytes_accessed=2 * rows * LANES, transcendentals=0
        ),
        name="point_weight",
    )(place, category_counts, shape_points, shape_category, mine)


def input_grad_kernel(grad_ref, w_ref, held_ref, *refs):
    out_ref, same_ref = refs[-2:]

    @pl.when(pl.program_id(0) == 0)
    def _():
        same_ref[...] = held_ref[...]

    out_ref[...] = dot(grad_ref[...], w_ref[...]).astype(BF16)


def input_grads(grads, weight, held, whole, tile, first, count):
    rows, width = grads.shape
    by_row = pl.BlockSpec((tile, width), lambda i: (i + first, 0))
    every = pl.BlockSpec(held.shape, lambda i: (0,) * held.ndim)
    more = [] if whole is None else [whole]
    return pl.pallas_call(
        input_grad_kernel,
        grid=(count,),
        in_specs=[by_row, pl.BlockSpec((width, width), lambda i: (0, 0)), every]
        + [pl.BlockSpec(memory_space=pl.ANY)] * len(more),
        out_specs=[by_row, every],
        out_shape=[
            jax.ShapeDtypeStruct((rows, width), BF16),
            jax.ShapeDtypeStruct(held.shape, held.dtype),
        ],
        input_output_aliases={3: 0} if more else {},
        cost_estimate=pl.CostEstimate(
            flops=2 * count * tile * width * width,
            bytes_accessed=4 * count * tile * width,
            transcendentals=0,
        ),
        compiler_params=pltpu.CompilerParams(vmem_limit_bytes=GRAD_VMEM),
        name="input_grad",
    )(grads, weight, held, *more)


def activate(half):
    lift = 1.0 + jnp.tanh(half)
    value = (half * lift).astype(BF16)
    lift = lift.astype(BF16)
    return value, lift + value * (jnp.asarray(2, BF16) - lift)


def layers_kernel(masks, parts, *refs):
    gathered = refs[1:9]
    place_ref = refs[0]
    sources = refs[9:12]
    out_hbm, grad_ref, wt_a, keep_ref, send_ref = refs[12:17]
    dir_a, dir_b, w_a, w_b, wt_b, gw_a, gw_b, vec, gsum, landed, columns, arrived = refs[17:29]
    held, out_held, came, left = refs[29:32], refs[32], refs[33], refs[34]
    step, steps = pl.program_id(0), pl.num_programs(0)
    tile, width = held[0].shape[1:]
    sub = tile // parts
    slot_now = lax.rem(step, 2)
    x_ref, cot_ref, pw_ref = [ref.at[slot_now] for ref in held]
    out_ref = out_held.at[slot_now]

    def fetches(index):
        rows = pl.ds(pl.multiple_of(index * tile, tile), tile)
        place = lax.rem(index, 2)
        return [
            pltpu.make_async_copy(source.at[rows, :], ref.at[place], came.at[k, place])
            for k, (source, ref) in enumerate(zip(sources, held))
        ]

    def leaving(index):
        rows = pl.ds(pl.multiple_of(index * tile, tile), tile)
        place = lax.rem(index, 2)
        return pltpu.make_async_copy(out_held.at[place], out_hbm.at[rows, :], left.at[place])

    @pl.when(step == 0)
    def _():
        for copy in fetches(0):
            copy.start()

    def owner(slot):
        return place_ref[0] ^ masks[slot]

    @pl.when(step == 0)
    def _():
        copies = [
            pltpu.make_async_copy(ref, landed.at[k], arrived.at[k])
            for k, ref in enumerate(gathered)
        ]
        for copy in copies:
            copy.start()
        for copy in copies:
            copy.wait()
        for slot in range(len(masks)):
            rows = pl.ds(pl.multiple_of(owner(slot) * SLOT, SLOT), SLOT)
            block = landed[slot // 4, slot % 4]
            dir_a[rows, :] = block[:, 0:width]
            dir_b[rows, :] = block[:, width : 2 * width]
            columns[rows, :] = block[:, 2 * width :].astype(F32)
        small = columns[...].T
        for k, (direction, w, wt) in enumerate(((dir_a, w_a, wt_a), (dir_b, w_b, wt_b))):
            full = direction[...].astype(F32)
            norm = lax.rsqrt(jnp.sum(full * full, axis=0, keepdims=True) + EPS)
            scale = small[2 * k : 2 * k + 1] * norm
            weight = (scale * full).astype(BF16)
            half = weight * jnp.asarray(0.5, BF16)
            w[...] = half
            wt[...] = (weight if k == 0 else half).T
            vec[3 * k : 3 * k + 1, :] = 0.5 * small[2 * k + 1 : 2 * k + 2]
            vec[3 * k + 1 : 3 * k + 2, :] = scale
            vec[3 * k + 2 : 3 * k + 3, :] = norm
        gw_a[...] = jnp.zeros_like(gw_a)
        gw_b[...] = jnp.zeros_like(gw_b)
        gsum[...] = jnp.zeros_like(gsum)

    @pl.when(step + 1 < steps)
    def _():
        for copy in fetches(step + 1):
            copy.start()

    @pl.when(step >= 2)
    def _():
        leaving(step - 2).wait()

    for copy in fetches(step):
        copy.wait()
    spans = [pl.ds(k * sub, sub) for k in range(parts)]
    hidden, slope_a = zip(
        *[activate(dot(x_ref[s, :], w_a[...]) + vec[0:1, :]) for s in spans]
    )
    grads = []
    for s, h in zip(spans, hidden):
        value, slope_b = activate(dot(h, w_b[...]) + vec[3:4, :])
        out_ref[s, :] = value
        weight = jnp.concatenate([pw_ref[s, :]] * (width // LANES), axis=1)
        grads.append((cot_ref[s, :] * weight) * slope_b)
    leaving(step).start()
    grads_a = [dot(g, wt_b[...]).astype(BF16) * sa for g, sa in zip(grads, slope_a)]
    for s, g in zip(spans, grads_a):
        grad_ref[s, :] = g
    ones = jnp.ones((SLOT, tile), BF16)
    join = lambda pieces: jnp.concatenate(pieces, axis=0)
    both = dot(join([join(hidden).T, ones]), join(grads))
    gw_b[...] += both[:width]
    gsum[8:16, :] += both[width : width + 8]
    both = dot(join([x_ref[...].T, ones]), join(grads_a))
    gw_a[...] += both[:width]
    gsum[0:8, :] += both[width : width + 8]

    @pl.when(step == steps - 1)
    def _():
        small = []
        for k, (direction, gw) in enumerate(((dir_a, gw_a), (dir_b, gw_b))):
            full = direction[...].astype(F32)
            grad = gw[...]
            scale, norm = vec[3 * k + 1 : 3 * k + 2, :], vec[3 * k + 2 : 3 * k + 3, :]
            inner = jnp.sum(grad * full, axis=0, keepdims=True)
            gw[...] = scale * grad - (scale * norm * norm * inner) * full
            small += [norm * inner, gsum[8 * k : 8 * k + 1, :]]
        gsum[0:8, :] = jnp.concatenate(small + [jnp.zeros((4, width), F32)], axis=0)
        for slot in range(len(masks)):
            home = owner(slot)
            rows = pl.ds(pl.multiple_of(home * SLOT, SLOT), SLOT)
            chunk = pl.ds(pl.multiple_of(home * SLOT // LANES * LANES, LANES), LANES)
            extra = pltpu.roll(gsum[0:8, chunk], LANES - home * SLOT % LANES, 1)
            extra = jnp.concatenate([extra, jnp.zeros((8, LANES), F32)], axis=0)
            block = jnp.concatenate([gw_a[rows, :], gw_b[rows, :], extra], axis=1)
            if slot < len(masks) // 2:
                keep_ref[slot] = block
            else:
                send_ref[slot - len(masks) // 2] = block.astype(BF16)

        @pl.when(steps > 1)
        def _():
            leaving(step - 1).wait()

        leaving(step).wait()


def layers(place, gathered, layer_input, cotangent, weights, masks):
    rows, width = layer_input.shape
    tile = pick_tile(rows)
    parts = 4 if tile % (4 * SLOT) == 0 else 1
    span = 2 * width + LANES
    half = len(masks) // 2
    by_row = lambda w: pl.BlockSpec((tile, w), lambda i: (i, 0))
    whole = lambda *dims: pl.BlockSpec(dims, lambda i: (0,) * len(dims))
    square = lambda dtype: pltpu.VMEM((width, width), dtype)
    return pl.pallas_call(
        functools.partial(layers_kernel, masks, parts),
        grid=(rows // tile,),
        in_specs=[pl.BlockSpec(memory_space=pltpu.SMEM)]
        + [pl.BlockSpec(memory_space=pl.ANY)] * 8
        + [pl.BlockSpec(memory_space=pl.ANY)] * 3,
        out_specs=[
            pl.BlockSpec(memory_space=pl.ANY),
            by_row(width),
            whole(width, width),
            whole(half, SLOT, span),
            whole(half, SLOT, span),
        ],
        out_shape=[
            jax.ShapeDtypeStruct((rows, width), BF16),
            pltpu.VMEM((rows, width), BF16),
            jax.ShapeDtypeStruct((width, width), BF16),
            jax.ShapeDtypeStruct((half, SLOT, span), F32),
            jax.ShapeDtypeStruct((half, SLOT, span), BF16),
        ],
        scratch_shapes=[square(BF16)] * 5
        + [square(F32)] * 2
        + [
            pltpu.VMEM((8, width), F32),
            pltpu.VMEM((16, width), F32),
            pltpu.VMEM((8, 4, SLOT, span), BF16),
            pltpu.VMEM((width, LANES), F32),
            pltpu.SemaphoreType.DMA((8,)),
            pltpu.VMEM((2, tile, width), BF16),
            pltpu.VMEM((2, tile, width), BF16),
            pltpu.VMEM((2, tile, LANES), BF16),
            pltpu.VMEM((2, tile, width), BF16),
            pltpu.SemaphoreType.DMA((3, 2)),
            pltpu.SemaphoreType.DMA((2,)),
        ],
        compiler_params=pltpu.CompilerParams(vmem_limit_bytes=VMEM_BYTES),
        name="layers",
    )(place, *gathered, layer_input, cotangent, weights)


def swap(value, mask, groups):
    return lax.ppermute(value, AXES, [(k, k ^ mask) for k in range(groups)])


def body(
    layer_input,
    cotangent,
    shape_points,
    shape_category,
    category_counts,
    dir_a,
    gain_a,
    bias_a,
    dir_b,
    gain_b,
    bias_b,
):
    dp, fsdp = lax.axis_size("dp"), lax.axis_size("fsdp")
    groups = dp * fsdp
    rows, width = layer_input.shape
    share = dir_a.shape[0]
    slots = width // SLOT
    average = groups * rows // shape_points.shape[0]
    me = lax.axis_index(AXES).astype(jnp.int32)
    fast = share == SLOT and groups == 32 and fsdp == 8
    small = jnp.stack([gain_a, bias_a, gain_b, bias_b])
    place = jnp.stack([me if fast else jnp.zeros_like(me), me * rows])
    weigh = lambda held: point_weights(
        place, shape_points, shape_category, category_counts, held, rows, average
    )
    if fast:
        extra = jnp.pad(small.T, ((0, 0), (0, LANES - 4)))
        mine = jnp.concatenate([dir_a, dir_b, extra], axis=1)[None]
        near = [mine] + [swap(mine, m, groups) for m in (2, 4, 6)]
        near = jnp.concatenate(near, axis=0)
        weights, same = weigh(near)
        wide = [same] + [swap(near, m, groups) for m in (1, 16, 17)]
        gathered = wide + [swap(v, 8, groups) for v in wide]
        masks = [c ^ xy ^ z for c in (0, 8) for xy in (0, 1, 16, 17) for z in (0, 2, 4, 6)]
    else:
        full = [lax.all_gather(v, AXES, axis=0, tiled=True) for v in (dir_a, dir_b)]
        vectors = lax.all_gather(small, AXES, axis=1, tiled=True)
        extra = jnp.pad(vectors.T.reshape(slots, SLOT, 4), ((0, 0), (0, 0), (0, LANES - 4)))
        blocks = [v.reshape(slots, SLOT, width) for v in full] + [extra]
        blocks = jnp.concatenate(blocks, axis=2)
        gathered = [blocks[4 * k : 4 * k + 4] for k in range(8)]
        masks = list(range(slots))
        weights, _ = weigh(dir_a)
    tile = pick_tile(rows)
    tiles = rows // tile
    first = tiles * 5 // 8
    layer_output, grads, weight, keep, send = layers(
        place, gathered, layer_input, cotangent, weights, masks
    )
    if fast:
        total = keep + swap(send, 8, groups).astype(F32)
        parts = [total[4 * k : 4 * k + 4] for k in range(4)]
        came = [swap(parts[k].astype(BF16), m, groups) for k, m in ((1, 1), (2, 16), (3, 17))]
        input_grad, held = input_grads(grads, weight, parts[0], None, tile, 0, first)
        total = held + sum(v.astype(F32) for v in came)
        came = [swap(total[k].astype(BF16), m, groups) for k, m in ((1, 2), (2, 4), (3, 6))]
        input_grad, held = input_grads(
            grads, weight, total[0], input_grad, tile, first, tiles - first
        )
        total = held + sum(v.astype(F32) for v in came)
        vectors = total[0:4, 2 * width : 2 * width + SLOT]
        grad_a, grad_b = total[:, :width], total[:, width : 2 * width]
    else:
        input_grad, _ = input_grads(grads, weight, keep[0], None, tile, 0, tiles)
        total = jnp.concatenate([keep, send.astype(F32)], axis=0)
        scatter = lambda v, d: lax.psum_scatter(v, AXES, scatter_dimension=d, tiled=True)
        square = total[:, :, : 2 * width].reshape(width, 2 * width)
        square = scatter(square, 0)
        grad_a, grad_b = square[:, :width], square[:, width:]
        vectors = total[:, 0:4, 2 * width : 2 * width + SLOT].transpose(1, 0, 2).reshape(4, width)
        vectors = scatter(vectors, 1)
    return (
        layer_output,
        input_grad,
        grad_a,
        vectors[0],
        vectors[1],
        grad_b,
        vectors[2],
        vectors[3],
    )


def solution(mesh):
    rows, row, none = P(AXES, None), P(AXES), P()
    in_specs = (rows, rows, none, none, none, rows, row, row, rows, row, row)
    out_specs = (rows, rows, rows, row, row, rows, row, row)
    return jax.shard_map(body, mesh=mesh, in_specs=in_specs, out_specs=out_specs, check_vma=False)
```

```python
import functools
import math

import jax
import jax.numpy as jnp
from jax import lax
from jax.experimental import pallas as pl
from jax.experimental.pallas import tpu as pltpu
from jax.sharding import PartitionSpec as P

AXES = ("dp", "fsdp")
EPS = 1e-06
SLOT = 16
LANES = 128
F32 = jnp.float32
BF16 = jnp.bfloat16
VMEM_BYTES = 36 << 20
BIG_TILE = 1792
PART = 256
GRAD_VMEM = 10 << 20


def pick_tile(rows):
    for tile in (1472, 736, 512, 368, 256, 128, 64, 32, 16):
        if rows % tile == 0:
            return tile
    return rows


def dot(left, right):
    return jnp.dot(left, right, preferred_element_type=F32)


def point_weight_kernel(average, place_ref, counts_ref, points_ref, category_ref, mine_ref, out_ref, same_ref):
    same_ref[...] = mine_ref[...]
    line = lax.broadcasted_iota(jnp.int32, out_ref.shape, 0)
    position = place_ref[1] + line * LANES + lax.broadcasted_iota(jnp.int32, out_ref.shape, 1)

    def enter(shape, carry):
        start, count, points = carry
        after = position >= start
        count = jnp.where(after, counts_ref[category_ref[shape]], count)
        points = jnp.where(after, points_ref[shape], points)
        return start + points_ref[shape], count, points

    zero = jnp.zeros(out_ref.shape, jnp.int32)
    shapes = points_ref.shape[0]
    _, count, points = lax.fori_loop(
        0, shapes, enter, (jnp.int32(0), zero, zero), unroll=math.gcd(shapes, 8)
    )
    out_ref[...] = (
        count.astype(F32) * (average / 8.0) / jnp.maximum(points, average // 2).astype(F32)
    )


def point_weights(place, shape_points, shape_category, category_counts, mine, rows, average):
    lines = -(-rows // LANES // 8) * 8
    return pl.pallas_call(
        functools.partial(point_weight_kernel, average),
        in_specs=[pl.BlockSpec(memory_space=pltpu.SMEM)] * 4
        + [pl.BlockSpec(memory_space=pltpu.VMEM)],
        out_specs=[pl.BlockSpec(memory_space=pltpu.VMEM)] * 2,
        out_shape=[
            jax.ShapeDtypeStruct((lines, LANES), F32),
            jax.ShapeDtypeStruct(mine.shape, mine.dtype),
        ],
        compiler_params=pltpu.CompilerParams(vmem_limit_bytes=8 << 20),
        cost_estimate=pl.CostEstimate(
            flops=50 * rows * LANES, bytes_accessed=2 * rows * LANES, transcendentals=0
        ),
        name="point_weight",
    )(place, category_counts, shape_points, shape_category, mine)


def input_grad_kernel(grad_ref, w_ref, held_ref, *refs):
    out_ref, same_ref = refs[-2:]

    @pl.when(pl.program_id(0) == 0)
    def _():
        same_ref[...] = held_ref[...]

    out_ref[...] = dot(grad_ref[...], w_ref[...]).astype(BF16)


def input_grads(grads, weight, held, whole, tile, first, count):
    rows, width = grads.shape
    by_row = pl.BlockSpec((tile, width), lambda i: (i + first, 0))
    every = pl.BlockSpec(held.shape, lambda i: (0,) * held.ndim)
    more = [] if whole is None else [whole]
    return pl.pallas_call(
        input_grad_kernel,
        grid=(count,),
        in_specs=[by_row, pl.BlockSpec((width, width), lambda i: (0, 0)), every]
        + [pl.BlockSpec(memory_space=pl.ANY)] * len(more),
        out_specs=[by_row, every],
        out_shape=[
            jax.ShapeDtypeStruct((rows, width), BF16),
            jax.ShapeDtypeStruct(held.shape, held.dtype),
        ],
        input_output_aliases={3: 0} if more else {},
        cost_estimate=pl.CostEstimate(
            flops=2 * count * tile * width * width,
            bytes_accessed=4 * count * tile * width,
            transcendentals=0,
        ),
        compiler_params=pltpu.CompilerParams(vmem_limit_bytes=GRAD_VMEM),
        name="input_grad",
    )(grads, weight, held, *more)


def activate(half):
    lift = 1.0 + jnp.tanh(half)
    value = (half * lift).astype(BF16)
    lift = lift.astype(BF16)
    return value, lift + value * (jnp.asarray(2, BF16) - lift)


def layers_kernel(masks, *refs):
    gathered = refs[1:9]
    place_ref = refs[0]
    sources, weight_ref = refs[9:11], refs[11]
    out_hbm, grad_out, wt_a, keep_ref, send_ref = refs[12:17]
    dir_a, dir_b, w_a, w_b, wt_b, gw_a, gw_b, vec, gsum, landed, columns, arrived = refs[17:29]
    held, leaving, came, left = refs[29:31], refs[31:33], refs[33], refs[34]
    tile, width = held[0].shape[1:]
    total = sources[0].shape[0]
    first = total % tile or tile
    count = (total - first) // tile

    def fetches(start, size, place):
        return [
            pltpu.make_async_copy(
                source.at[pl.ds(start, size), :],
                ref.at[place, pl.ds(0, size), :],
                came.at[k, place],
            )
            for k, (source, ref) in enumerate(zip(sources, held))
        ]

    def leaves(start, size, place):
        return [
            pltpu.make_async_copy(
                ref.at[place, pl.ds(0, size), :],
                target.at[pl.ds(start, size), :],
                left.at[k, place],
            )
            for k, (ref, target) in enumerate(zip(leaving, (out_hbm, grad_out)))
        ]

    def start_of(index):
        return pl.multiple_of(first + (index - 1) * tile, SLOT)

    def begin(copies):
        for copy in copies:
            copy.start()

    def finish(copies):
        for copy in copies:
            copy.wait()

    begin(fetches(0, first, 0))

    def owner(slot):
        return place_ref[0] ^ masks[slot]

    copies = [
        pltpu.make_async_copy(ref, landed.at[k], arrived.at[k])
        for k, ref in enumerate(gathered)
    ]
    for copy in copies:
        copy.start()
    for copy in copies:
        copy.wait()
    for slot in range(len(masks)):
        rows = pl.ds(pl.multiple_of(owner(slot) * SLOT, SLOT), SLOT)
        block = landed[slot // 4, slot % 4]
        dir_a[rows, :] = block[:, 0:width]
        dir_b[rows, :] = block[:, width : 2 * width]
        columns[rows, :] = block[:, 2 * width :].astype(F32)
    small = columns[...].T
    for k, (direction, w, wt) in enumerate(((dir_a, w_a, wt_a), (dir_b, w_b, wt_b))):
        full = direction[...].astype(F32)
        norm = lax.rsqrt(jnp.sum(full * full, axis=0, keepdims=True) + EPS)
        scale = small[2 * k : 2 * k + 1] * norm
        weight = (scale * full).astype(BF16)
        half = weight * jnp.asarray(0.5, BF16)
        w[...] = half
        wt[...] = (weight if k == 0 else half).T
        vec[3 * k : 3 * k + 1, :] = 0.5 * small[2 * k + 1 : 2 * k + 2]
        vec[3 * k + 1 : 3 * k + 2, :] = scale
        vec[3 * k + 2 : 3 * k + 3, :] = norm
    gw_a[...] = jnp.zeros_like(gw_a)
    gw_b[...] = jnp.zeros_like(gw_b)
    gsum[...] = jnp.zeros_like(gsum)

    join = lambda pieces: jnp.concatenate(pieces, axis=0)

    def work(line, size, place):
        x_ref, cot_ref, out_ref, grad_ref = [ref.at[place] for ref in (*held, *leaving)]
        whole = pl.ds(0, size)
        spans = [pl.ds(k, min(PART, size - k)) for k in range(0, size, PART)]
        hidden, slope_a = zip(
            *[activate(dot(x_ref[s, :], w_a[...]) + vec[0:1, :]) for s in spans]
        )
        grads = []
        for s, h in zip(spans, hidden):
            value, slope_b = activate(dot(h, w_b[...]) + vec[3:4, :])
            out_ref[s, :] = value
            rows = [
                jnp.broadcast_to(weight_ref[pl.ds(line + k, 1), :], (LANES, LANES))
                for k in range(s.start // LANES, (s.start + s.size) // LANES)
            ]
            weight = join([row.T.astype(BF16) for row in rows])
            weight = jnp.concatenate([weight] * (width // LANES), axis=1)
            grads.append((cot_ref[s, :] * weight) * slope_b)
        grads_a = [dot(g, wt_b[...]).astype(BF16) * sa for g, sa in zip(grads, slope_a)]
        for s, g in zip(spans, grads_a):
            grad_ref[s, :] = g
        ones = jnp.ones((SLOT, size), BF16)
        both = dot(join([join(hidden).T, ones]), join(grads))
        gw_b[...] += both[:width]
        gsum[8:16, :] += both[width : width + 8]
        both = dot(join([x_ref[whole, :].T, ones]), grad_ref[whole, :])
        gw_a[...] += both[:width]
        gsum[0:8, :] += both[width : width + 8]

    if count:
        begin(fetches(start_of(1), tile, 1))
    finish(fetches(0, first, 0))
    work(0, first, 0)
    begin(leaves(0, first, 0))

    def turn(index, carry):
        place = lax.rem(index, 2)

        @pl.when(index < count)
        def _():
            begin(fetches(start_of(index + 1), tile, 1 - place))

        @pl.when(index == 2)
        def _():
            finish(leaves(0, first, 0))

        @pl.when(index > 2)
        def _():
            finish(leaves(start_of(index - 2), tile, place))

        finish(fetches(start_of(index), tile, place))
        work(start_of(index) // LANES, tile, place)
        begin(leaves(start_of(index), tile, place))
        return carry

    lax.fori_loop(1, count + 1, turn, 0)

    small = []
    for k, (direction, gw) in enumerate(((dir_a, gw_a), (dir_b, gw_b))):
        full = direction[...].astype(F32)
        grad = gw[...]
        scale, norm = vec[3 * k + 1 : 3 * k + 2, :], vec[3 * k + 2 : 3 * k + 3, :]
        inner = jnp.sum(grad * full, axis=0, keepdims=True)
        gw[...] = scale * grad - (scale * norm * norm * inner) * full
        small += [norm * inner, gsum[8 * k : 8 * k + 1, :]]
    gsum[0:8, :] = jnp.concatenate(small + [jnp.zeros((4, width), F32)], axis=0)
    for slot in range(len(masks)):
        home = owner(slot)
        rows = pl.ds(pl.multiple_of(home * SLOT, SLOT), SLOT)
        chunk = pl.ds(pl.multiple_of(home * SLOT // LANES * LANES, LANES), LANES)
        extra = pltpu.roll(gsum[0:8, chunk], LANES - home * SLOT % LANES, 1)
        extra = jnp.concatenate([extra, jnp.zeros((8, LANES), F32)], axis=0)
        block = jnp.concatenate([gw_a[rows, :], gw_b[rows, :], extra], axis=1)
        if slot < len(masks) // 2:
            keep_ref[slot] = block
        else:
            send_ref[slot - len(masks) // 2] = block.astype(BF16)

    if count < 2:
        finish(leaves(0, first, 0))
    for index in range(max(1, count - 1), count + 1):
        finish(leaves(start_of(index), tile, index % 2))


def layers(place, gathered, layer_input, cotangent, weights, masks):
    rows, width = layer_input.shape
    tile = min(BIG_TILE, rows)
    span = 2 * width + LANES
    half = len(masks) // 2
    square = lambda dtype: pltpu.VMEM((width, width), dtype)
    return pl.pallas_call(
        functools.partial(layers_kernel, masks),
        in_specs=[pl.BlockSpec(memory_space=pltpu.SMEM)]
        + [pl.BlockSpec(memory_space=pl.ANY)] * 8
        + [pl.BlockSpec(memory_space=pl.ANY)] * 2
        + [pl.BlockSpec(memory_space=pltpu.VMEM)],
        out_specs=[
            pl.BlockSpec(memory_space=pl.ANY),
            pl.BlockSpec(memory_space=pl.ANY),
            pl.BlockSpec(memory_space=pltpu.VMEM),
            pl.BlockSpec(memory_space=pltpu.VMEM),
            pl.BlockSpec(memory_space=pltpu.VMEM),
        ],
        out_shape=[
            jax.ShapeDtypeStruct((rows, width), BF16),
            pltpu.VMEM((rows, width), BF16),
            jax.ShapeDtypeStruct((width, width), BF16),
            jax.ShapeDtypeStruct((half, SLOT, span), F32),
            jax.ShapeDtypeStruct((half, SLOT, span), BF16),
        ],
        scratch_shapes=[square(BF16)] * 5
        + [square(F32)] * 2
        + [
            pltpu.VMEM((8, width), F32),
            pltpu.VMEM((16, width), F32),
            pltpu.VMEM((8, 4, SLOT, span), BF16),
            pltpu.VMEM((width, LANES), F32),
            pltpu.SemaphoreType.DMA((8,)),
            pltpu.VMEM((2, tile, width), BF16),
            pltpu.VMEM((2, tile, width), BF16),
            pltpu.VMEM((2, tile, width), BF16),
            pltpu.VMEM((2, tile, width), BF16),
            pltpu.SemaphoreType.DMA((2, 2)),
            pltpu.SemaphoreType.DMA((2, 2)),
        ],
        compiler_params=pltpu.CompilerParams(vmem_limit_bytes=VMEM_BYTES),
        name="layers",
    )(place, *gathered, layer_input, cotangent, weights)


def swap(value, mask, groups):
    return lax.ppermute(value, AXES, [(k, k ^ mask) for k in range(groups)])


def body(
    layer_input,
    cotangent,
    shape_points,
    shape_category,
    category_counts,
    dir_a,
    gain_a,
    bias_a,
    dir_b,
    gain_b,
    bias_b,
):
    dp, fsdp = lax.axis_size("dp"), lax.axis_size("fsdp")
    groups = dp * fsdp
    rows, width = layer_input.shape
    share = dir_a.shape[0]
    slots = width // SLOT
    average = groups * rows // shape_points.shape[0]
    me = lax.axis_index(AXES).astype(jnp.int32)
    fast = share == SLOT and groups == 32 and fsdp == 8
    small = jnp.stack([gain_a, bias_a, gain_b, bias_b])
    place = jnp.stack([me if fast else jnp.zeros_like(me), me * rows])
    weigh = lambda held: point_weights(
        place, shape_points, shape_category, category_counts, held, rows, average
    )
    if fast:
        extra = jnp.pad(small.T, ((0, 0), (0, LANES - 4)))
        mine = jnp.concatenate([dir_a, dir_b, extra], axis=1)[None]
        near = [mine] + [swap(mine, m, groups) for m in (2, 4, 6)]
        near = jnp.concatenate(near, axis=0)
        weights, same = weigh(near)
        wide = [same] + [swap(near, m, groups) for m in (1, 16, 17)]
        gathered = wide + [swap(v, 8, groups) for v in wide]
        masks = [c ^ xy ^ z for c in (0, 8) for xy in (0, 1, 16, 17) for z in (0, 2, 4, 6)]
    else:
        full = [lax.all_gather(v, AXES, axis=0, tiled=True) for v in (dir_a, dir_b)]
        vectors = lax.all_gather(small, AXES, axis=1, tiled=True)
        extra = jnp.pad(vectors.T.reshape(slots, SLOT, 4), ((0, 0), (0, 0), (0, LANES - 4)))
        blocks = [v.reshape(slots, SLOT, width) for v in full] + [extra]
        blocks = jnp.concatenate(blocks, axis=2)
        gathered = [blocks[4 * k : 4 * k + 4] for k in range(8)]
        masks = list(range(slots))
        weights, _ = weigh(dir_a)
    tile = pick_tile(rows)
    tiles = rows // tile
    first = tiles * 5 // 8
    layer_output, grads, weight, keep, send = layers(
        place, gathered, layer_input, cotangent, weights, masks
    )
    if fast:
        total = keep + swap(send, 8, groups).astype(F32)
        parts = [total[4 * k : 4 * k + 4] for k in range(4)]
        came = [swap(parts[k].astype(BF16), m, groups) for k, m in ((1, 1), (2, 16), (3, 17))]
        input_grad, held = input_grads(grads, weight, parts[0], None, tile, 0, first)
        total = held + sum(v.astype(F32) for v in came)
        came = [swap(total[k].astype(BF16), m, groups) for k, m in ((1, 2), (2, 4), (3, 6))]
        input_grad, held = input_grads(
            grads, weight, total[0], input_grad, tile, first, tiles - first
        )
        total = held + sum(v.astype(F32) for v in came)
        vectors = total[0:4, 2 * width : 2 * width + SLOT]
        grad_a, grad_b = total[:, :width], total[:, width : 2 * width]
    else:
        input_grad, _ = input_grads(grads, weight, keep[0], None, tile, 0, tiles)
        total = jnp.concatenate([keep, send.astype(F32)], axis=0)
        scatter = lambda v, d: lax.psum_scatter(v, AXES, scatter_dimension=d, tiled=True)
        square = total[:, :, : 2 * width].reshape(width, 2 * width)
        square = scatter(square, 0)
        grad_a, grad_b = square[:, :width], square[:, width:]
        vectors = total[:, 0:4, 2 * width : 2 * width + SLOT].transpose(1, 0, 2).reshape(4, width)
        vectors = scatter(vectors, 1)
    return (
        layer_output,
        input_grad,
        grad_a,
        vectors[0],
        vectors[1],
        grad_b,
        vectors[2],
        vectors[3],
    )


def solution(mesh):
    rows, row, none = P(AXES, None), P(AXES), P()
    in_specs = (rows, rows, none, none, none, rows, row, row, rows, row, row)
    out_specs = (rows, rows, rows, row, row, rows, row, row)
    return jax.shard_map(body, mesh=mesh, in_specs=in_specs, out_specs=out_specs, check_vma=False)
```

```python
import functools
import math

import jax
import jax.numpy as jnp
from jax import lax
from jax.experimental import pallas as pl
from jax.experimental.pallas import tpu as pltpu
from jax.sharding import PartitionSpec as P

AXES = ("dp", "fsdp")
EPS = 1e-06
SLOT = 16
LANES = 128
F32 = jnp.float32
BF16 = jnp.bfloat16
VMEM_BYTES = 36 << 20
BIG_TILE = 1792
PART = 256
GRAD_VMEM = 10 << 20


def pick_tile(rows):
    for tile in (1472, 736, 512, 368, 256, 128, 64, 32, 16):
        if rows % tile == 0:
            return tile
    return rows


def dot(left, right):
    return jnp.dot(left, right, preferred_element_type=F32)


def point_weight_kernel(average, place_ref, counts_ref, points_ref, category_ref, mine_ref, out_ref, same_ref):
    same_ref[...] = mine_ref[...]
    line = lax.broadcasted_iota(jnp.int32, out_ref.shape, 0)
    position = place_ref[1] + line * LANES + lax.broadcasted_iota(jnp.int32, out_ref.shape, 1)

    def enter(shape, carry):
        start, count, points = carry
        after = position >= start
        count = jnp.where(after, counts_ref[category_ref[shape]], count)
        points = jnp.where(after, points_ref[shape], points)
        return start + points_ref[shape], count, points

    zero = jnp.zeros(out_ref.shape, jnp.int32)
    shapes = points_ref.shape[0]
    _, count, points = lax.fori_loop(
        0, shapes, enter, (jnp.int32(0), zero, zero), unroll=math.gcd(shapes, 8)
    )
    out_ref[...] = (
        count.astype(F32) * (average / 8.0) / jnp.maximum(points, average // 2).astype(F32)
    )


def point_weights(place, shape_points, shape_category, category_counts, mine, rows, average):
    lines = -(-rows // LANES // 8) * 8
    return pl.pallas_call(
        functools.partial(point_weight_kernel, average),
        in_specs=[pl.BlockSpec(memory_space=pltpu.SMEM)] * 4
        + [pl.BlockSpec(memory_space=pltpu.VMEM)],
        out_specs=[pl.BlockSpec(memory_space=pltpu.VMEM)] * 2,
        out_shape=[
            jax.ShapeDtypeStruct((lines, LANES), F32),
            jax.ShapeDtypeStruct(mine.shape, mine.dtype),
        ],
        compiler_params=pltpu.CompilerParams(vmem_limit_bytes=8 << 20),
        cost_estimate=pl.CostEstimate(
            flops=50 * rows * LANES, bytes_accessed=2 * rows * LANES, transcendentals=0
        ),
        name="point_weight",
    )(place, category_counts, shape_points, shape_category, mine)


def input_grad_kernel(grad_ref, w_ref, held_ref, *refs):
    out_ref, same_ref = refs[-2:]

    @pl.when(pl.program_id(0) == 0)
    def _():
        same_ref[...] = held_ref[...]

    out_ref[...] = dot(grad_ref[...], w_ref[...]).astype(BF16)


def input_grads(grads, weight, held, whole, tile, first, count):
    rows, width = grads.shape
    by_row = pl.BlockSpec((tile, width), lambda i: (i + first, 0))
    every = pl.BlockSpec(held.shape, lambda i: (0,) * held.ndim)
    more = [] if whole is None else [whole]
    return pl.pallas_call(
        input_grad_kernel,
        grid=(count,),
        in_specs=[by_row, pl.BlockSpec((width, width), lambda i: (0, 0)), every]
        + [pl.BlockSpec(memory_space=pl.ANY)] * len(more),
        out_specs=[by_row, every],
        out_shape=[
            jax.ShapeDtypeStruct((rows, width), BF16),
            jax.ShapeDtypeStruct(held.shape, held.dtype),
        ],
        input_output_aliases={3: 0} if more else {},
        cost_estimate=pl.CostEstimate(
            flops=2 * count * tile * width * width,
            bytes_accessed=4 * count * tile * width,
            transcendentals=0,
        ),
        compiler_params=pltpu.CompilerParams(vmem_limit_bytes=GRAD_VMEM),
        name="input_grad",
    )(grads, weight, held, *more)


def activate(half, exact):
    lift = 1.0 + jnp.tanh(half)
    value = half * lift
    if exact:
        return value.astype(BF16), lift + value * (2.0 - lift)
    value, lift = value.astype(BF16), lift.astype(BF16)
    return value, lift + value * (jnp.asarray(2, BF16) - lift)


def layers_kernel(masks, *refs):
    gathered = refs[1:9]
    place_ref = refs[0]
    sources, weight_ref = refs[9:11], refs[11]
    out_hbm, grad_out, wt_a, keep_ref, send_ref = refs[12:17]
    dir_a, dir_b, w_a, w_b, wt_b, gw_a, gw_b, vec, gsum, landed, columns, arrived = refs[17:29]
    held, leaving, came, left = refs[29:31], refs[31:33], refs[33], refs[34]
    tile, width = held[0].shape[1:]
    total = sources[0].shape[0]
    first = total % tile or tile
    count = (total - first) // tile

    def fetches(start, size, place):
        return [
            pltpu.make_async_copy(
                source.at[pl.ds(start, size), :],
                ref.at[place, pl.ds(0, size), :],
                came.at[k, place],
            )
            for k, (source, ref) in enumerate(zip(sources, held))
        ]

    def leaves(start, size, place):
        return [
            pltpu.make_async_copy(
                ref.at[place, pl.ds(0, size), :],
                target.at[pl.ds(start, size), :],
                left.at[k, place],
            )
            for k, (ref, target) in enumerate(zip(leaving, (out_hbm, grad_out)))
        ]

    def start_of(index):
        return pl.multiple_of(first + (index - 1) * tile, SLOT)

    def begin(copies):
        for copy in copies:
            copy.start()

    def finish(copies):
        for copy in copies:
            copy.wait()

    begin(fetches(0, first, 0))

    def owner(slot):
        return place_ref[0] ^ masks[slot]

    copies = [
        pltpu.make_async_copy(ref, landed.at[k], arrived.at[k])
        for k, ref in enumerate(gathered)
    ]
    for copy in copies:
        copy.start()
    for copy in copies:
        copy.wait()
    for slot in range(len(masks)):
        rows = pl.ds(pl.multiple_of(owner(slot) * SLOT, SLOT), SLOT)
        block = landed[slot // 4, slot % 4]
        dir_a[rows, :] = block[:, 0:width]
        dir_b[rows, :] = block[:, width : 2 * width]
        columns[rows, :] = block[:, 2 * width :].astype(F32)
    small = columns[...].T
    for k, (direction, w, wt) in enumerate(((dir_a, w_a, wt_a), (dir_b, w_b, wt_b))):
        full = direction[...].astype(F32)
        norm = lax.rsqrt(jnp.sum(full * full, axis=0, keepdims=True) + EPS)
        scale = small[2 * k : 2 * k + 1] * norm
        weight = (scale * full).astype(BF16)
        half = weight * jnp.asarray(0.5, BF16)
        w[...] = half
        wt[...] = (weight if k == 0 else half).T
        vec[3 * k : 3 * k + 1, :] = 0.5 * small[2 * k + 1 : 2 * k + 2]
        vec[3 * k + 1 : 3 * k + 2, :] = scale
        vec[3 * k + 2 : 3 * k + 3, :] = norm
    gw_a[...] = jnp.zeros_like(gw_a)
    gw_b[...] = jnp.zeros_like(gw_b)
    gsum[...] = jnp.zeros_like(gsum)

    join = lambda pieces: jnp.concatenate(pieces, axis=0)

    def work(line, size, place):
        x_ref, cot_ref, out_ref, grad_ref = [ref.at[place] for ref in (*held, *leaving)]
        whole = pl.ds(0, size)
        spans = [pl.ds(k, min(PART, size - k)) for k in range(0, size, PART)]
        hidden, slope_a = zip(
            *[activate(dot(x_ref[s, :], w_a[...]) + vec[0:1, :], True) for s in spans]
        )
        slope_a = [v.astype(BF16) for v in slope_a]
        grads = []
        for s, h in zip(spans, hidden):
            value, slope_b = activate(dot(h, w_b[...]) + vec[3:4, :], True)
            out_ref[s, :] = value
            rows = [
                jnp.broadcast_to(weight_ref[pl.ds(line + k, 1), :], (LANES, LANES))
                for k in range(s.start // LANES, (s.start + s.size) // LANES)
            ]
            weight = join([row.T for row in rows])
            weight = jnp.concatenate([weight] * (width // LANES), axis=1)
            grads.append(cot_ref[s, :] * (weight * slope_b).astype(BF16))
        grads_a = [
            (dot(g, wt_b[...]) * sa.astype(F32)).astype(BF16) for g, sa in zip(grads, slope_a)
        ]
        for s, g in zip(spans, grads_a):
            grad_ref[s, :] = g
        ones = jnp.ones((SLOT, size), BF16)
        both = dot(join([join(hidden).T, ones]), join(grads))
        gw_b[...] += both[:width]
        gsum[8:16, :] += both[width : width + 8]
        both = dot(join([x_ref[whole, :].T, ones]), grad_ref[whole, :])
        gw_a[...] += both[:width]
        gsum[0:8, :] += both[width : width + 8]

    if count:
        begin(fetches(start_of(1), tile, 1))
    finish(fetches(0, first, 0))
    work(0, first, 0)
    begin(leaves(0, first, 0))

    def turn(index, carry):
        place = lax.rem(index, 2)

        @pl.when(index < count)
        def _():
            begin(fetches(start_of(index + 1), tile, 1 - place))

        @pl.when(index == 2)
        def _():
            finish(leaves(0, first, 0))

        @pl.when(index > 2)
        def _():
            finish(leaves(start_of(index - 2), tile, place))

        finish(fetches(start_of(index), tile, place))
        work(start_of(index) // LANES, tile, place)
        begin(leaves(start_of(index), tile, place))
        return carry

    lax.fori_loop(1, count + 1, turn, 0)

    small = []
    for k, (direction, gw) in enumerate(((dir_a, gw_a), (dir_b, gw_b))):
        full = direction[...].astype(F32)
        grad = gw[...]
        scale, norm = vec[3 * k + 1 : 3 * k + 2, :], vec[3 * k + 2 : 3 * k + 3, :]
        inner = jnp.sum(grad * full, axis=0, keepdims=True)
        gw[...] = scale * grad - (scale * norm * norm * inner) * full
        small += [norm * inner, gsum[8 * k : 8 * k + 1, :]]
    gsum[0:8, :] = jnp.concatenate(small + [jnp.zeros((4, width), F32)], axis=0)
    for slot in range(len(masks)):
        home = owner(slot)
        rows = pl.ds(pl.multiple_of(home * SLOT, SLOT), SLOT)
        chunk = pl.ds(pl.multiple_of(home * SLOT // LANES * LANES, LANES), LANES)
        extra = pltpu.roll(gsum[0:8, chunk], LANES - home * SLOT % LANES, 1)
        extra = jnp.concatenate([extra, jnp.zeros((8, LANES), F32)], axis=0)
        block = jnp.concatenate([gw_a[rows, :], gw_b[rows, :], extra], axis=1)
        if slot < len(masks) // 2:
            keep_ref[slot] = block
        else:
            send_ref[slot - len(masks) // 2] = block.astype(BF16)

    if count < 2:
        finish(leaves(0, first, 0))
    for index in range(max(1, count - 1), count + 1):
        finish(leaves(start_of(index), tile, index % 2))


def layers(place, gathered, layer_input, cotangent, weights, masks):
    rows, width = layer_input.shape
    tile = min(BIG_TILE, rows)
    span = 2 * width + LANES
    half = len(masks) // 2
    square = lambda dtype: pltpu.VMEM((width, width), dtype)
    return pl.pallas_call(
        functools.partial(layers_kernel, masks),
        in_specs=[pl.BlockSpec(memory_space=pltpu.SMEM)]
        + [pl.BlockSpec(memory_space=pl.ANY)] * 8
        + [pl.BlockSpec(memory_space=pl.ANY)] * 2
        + [pl.BlockSpec(memory_space=pltpu.VMEM)],
        out_specs=[
            pl.BlockSpec(memory_space=pl.ANY),
            pl.BlockSpec(memory_space=pl.ANY),
            pl.BlockSpec(memory_space=pltpu.VMEM),
            pl.BlockSpec(memory_space=pltpu.VMEM),
            pl.BlockSpec(memory_space=pltpu.VMEM),
        ],
        out_shape=[
            jax.ShapeDtypeStruct((rows, width), BF16),
            pltpu.VMEM((rows, width), BF16),
            jax.ShapeDtypeStruct((width, width), BF16),
            jax.ShapeDtypeStruct((half, SLOT, span), F32),
            jax.ShapeDtypeStruct((half, SLOT, span), BF16),
        ],
        scratch_shapes=[square(BF16)] * 5
        + [square(F32)] * 2
        + [
            pltpu.VMEM((8, width), F32),
            pltpu.VMEM((16, width), F32),
            pltpu.VMEM((8, 4, SLOT, span), BF16),
            pltpu.VMEM((width, LANES), F32),
            pltpu.SemaphoreType.DMA((8,)),
            pltpu.VMEM((2, tile, width), BF16),
            pltpu.VMEM((2, tile, width), BF16),
            pltpu.VMEM((2, tile, width), BF16),
            pltpu.VMEM((2, tile, width), BF16),
            pltpu.SemaphoreType.DMA((2, 2)),
            pltpu.SemaphoreType.DMA((2, 2)),
        ],
        compiler_params=pltpu.CompilerParams(vmem_limit_bytes=VMEM_BYTES),
        name="layers",
    )(place, *gathered, layer_input, cotangent, weights)


def swap(value, mask, groups):
    return lax.ppermute(value, AXES, [(k, k ^ mask) for k in range(groups)])


def body(
    layer_input,
    cotangent,
    shape_points,
    shape_category,
    category_counts,
    dir_a,
    gain_a,
    bias_a,
    dir_b,
    gain_b,
    bias_b,
):
    dp, fsdp = lax.axis_size("dp"), lax.axis_size("fsdp")
    groups = dp * fsdp
    rows, width = layer_input.shape
    share = dir_a.shape[0]
    slots = width // SLOT
    average = groups * rows // shape_points.shape[0]
    me = lax.axis_index(AXES).astype(jnp.int32)
    fast = share == SLOT and groups == 32 and fsdp == 8
    small = jnp.stack([gain_a, bias_a, gain_b, bias_b])
    place = jnp.stack([me if fast else jnp.zeros_like(me), me * rows])
    weigh = lambda held: point_weights(
        place, shape_points, shape_category, category_counts, held, rows, average
    )
    if fast:
        span = 2 * width + LANES
        lane = lax.broadcasted_iota(jnp.int32, (share, span), 1)
        mine = jnp.pad(dir_a, ((0, 0), (0, span - width)))
        late = jnp.pad(dir_b, ((0, 0), (width, span - 2 * width)))
        mine = jnp.where(lane < width, mine, late)
        for k, vector in enumerate((gain_a, bias_a, gain_b, bias_b)):
            mine = jnp.where(lane == 2 * width + k, vector[:, None], mine)
        mine = mine[None]
        near = [mine] + [swap(mine, m, groups) for m in (2, 4, 6)]
        near = jnp.concatenate(near, axis=0)
        weights, same = weigh(near)
        wide = [same] + [swap(near, m, groups) for m in (1, 16, 17)]
        gathered = wide + [swap(v, 8, groups) for v in wide]
        masks = [c ^ xy ^ z for c in (0, 8) for xy in (0, 1, 16, 17) for z in (0, 2, 4, 6)]
    else:
        full = [lax.all_gather(v, AXES, axis=0, tiled=True) for v in (dir_a, dir_b)]
        vectors = lax.all_gather(small, AXES, axis=1, tiled=True)
        extra = jnp.pad(vectors.T.reshape(slots, SLOT, 4), ((0, 0), (0, 0), (0, LANES - 4)))
        blocks = [v.reshape(slots, SLOT, width) for v in full] + [extra]
        blocks = jnp.concatenate(blocks, axis=2)
        gathered = [blocks[4 * k : 4 * k + 4] for k in range(8)]
        masks = list(range(slots))
        weights, _ = weigh(dir_a)
    tile = pick_tile(rows)
    tiles = rows // tile
    first = tiles * 5 // 8
    layer_output, grads, weight, keep, send = layers(
        place, gathered, layer_input, cotangent, weights, masks
    )
    if fast:
        total = keep + swap(send, 8, groups).astype(F32)
        parts = [total[4 * k : 4 * k + 4] for k in range(4)]
        came = [swap(parts[k].astype(BF16), m, groups) for k, m in ((1, 1), (2, 16), (3, 17))]
        input_grad, held = input_grads(grads, weight, parts[0], None, tile, 0, first)
        total = held + sum(v.astype(F32) for v in came)
        came = [swap(total[k].astype(BF16), m, groups) for k, m in ((1, 2), (2, 4), (3, 6))]
        input_grad, held = input_grads(
            grads, weight, total[0], input_grad, tile, first, tiles - first
        )
        total = held + sum(v.astype(F32) for v in came)
        vectors = total[0:4, 2 * width : 2 * width + SLOT]
        grad_a, grad_b = total[:, :width], total[:, width : 2 * width]
    else:
        input_grad, _ = input_grads(grads, weight, keep[0], None, tile, 0, tiles)
        total = jnp.concatenate([keep, send.astype(F32)], axis=0)
        scatter = lambda v, d: lax.psum_scatter(v, AXES, scatter_dimension=d, tiled=True)
        square = total[:, :, : 2 * width].reshape(width, 2 * width)
        square = scatter(square, 0)
        grad_a, grad_b = square[:, :width], square[:, width:]
        vectors = total[:, 0:4, 2 * width : 2 * width + SLOT].transpose(1, 0, 2).reshape(4, width)
        vectors = scatter(vectors, 1)
    return (
        layer_output,
        input_grad,
        grad_a,
        vectors[0],
        vectors[1],
        grad_b,
        vectors[2],
        vectors[3],
    )


def solution(mesh):
    rows, row, none = P(AXES, None), P(AXES), P()
    in_specs = (rows, rows, none, none, none, rows, row, row, rows, row, row)
    out_specs = (rows, rows, rows, row, row, rows, row, row)
    return jax.shard_map(body, mesh=mesh, in_specs=in_specs, out_specs=out_specs, check_vma=False)
```

```python
import functools
import math

import jax
import jax.numpy as jnp
from jax import lax
from jax.experimental import pallas as pl
from jax.experimental.pallas import tpu as pltpu
from jax.sharding import PartitionSpec as P

AXES = ("dp", "fsdp")
EPS = 1e-06
SLOT = 16
LANES = 128
F32 = jnp.float32
BF16 = jnp.bfloat16
VMEM_BYTES = 36 << 20
BIG_TILE = 1792
PART = 256
STRIP = 64
GRAD_VMEM = 10 << 20


def pick_tile(rows):
    for tile in (1472, 736, 512, 368, 256, 128, 64, 32, 16):
        if rows % tile == 0:
            return tile
    return rows


def dot(left, right):
    return jnp.dot(left, right, preferred_element_type=F32)


def point_weight_kernel(average, place_ref, counts_ref, points_ref, category_ref, mine_ref, out_ref, same_ref):
    same_ref[...] = mine_ref[...]
    line = lax.broadcasted_iota(jnp.int32, out_ref.shape, 0)
    position = place_ref[1] + line * LANES + lax.broadcasted_iota(jnp.int32, out_ref.shape, 1)

    def enter(shape, carry):
        start, count, points = carry
        after = position >= start
        count = jnp.where(after, counts_ref[category_ref[shape]], count)
        points = jnp.where(after, points_ref[shape], points)
        return start + points_ref[shape], count, points

    zero = jnp.zeros(out_ref.shape, jnp.int32)
    shapes = points_ref.shape[0]
    _, count, points = lax.fori_loop(
        0, shapes, enter, (jnp.int32(0), zero, zero), unroll=math.gcd(shapes, 8)
    )
    out_ref[...] = (
        count.astype(F32) * (average / 8.0) / jnp.maximum(points, average // 2).astype(F32)
    )


def point_weights(place, shape_points, shape_category, category_counts, mine, rows, average):
    lines = -(-rows // LANES // 8) * 8
    return pl.pallas_call(
        functools.partial(point_weight_kernel, average),
        in_specs=[pl.BlockSpec(memory_space=pltpu.SMEM)] * 4
        + [pl.BlockSpec(memory_space=pltpu.VMEM)],
        out_specs=[pl.BlockSpec(memory_space=pltpu.VMEM)] * 2,
        out_shape=[
            jax.ShapeDtypeStruct((lines, LANES), F32),
            jax.ShapeDtypeStruct(mine.shape, mine.dtype),
        ],
        compiler_params=pltpu.CompilerParams(vmem_limit_bytes=8 << 20),
        cost_estimate=pl.CostEstimate(
            flops=50 * rows * LANES, bytes_accessed=2 * rows * LANES, transcendentals=0
        ),
        name="point_weight",
    )(place, category_counts, shape_points, shape_category, mine)


def input_grad_kernel(grad_ref, w_ref, held_ref, *refs):
    out_ref, same_ref = refs[-2:]

    @pl.when(pl.program_id(0) == 0)
    def _():
        same_ref[...] = held_ref[...]

    out_ref[...] = lax.dot_general(
        grad_ref[...], w_ref[...], (((1,), (1,)), ((), ())), preferred_element_type=F32
    ).astype(BF16)


def input_grads(grads, weight, held, whole, tile, first, count):
    rows, width = grads.shape
    by_row = pl.BlockSpec((tile, width), lambda i: (i + first, 0))
    every = pl.BlockSpec(held.shape, lambda i: (0,) * held.ndim)
    more = [] if whole is None else [whole]
    return pl.pallas_call(
        input_grad_kernel,
        grid=(count,),
        in_specs=[by_row, pl.BlockSpec((width, width), lambda i: (0, 0)), every]
        + [pl.BlockSpec(memory_space=pl.ANY)] * len(more),
        out_specs=[by_row, every],
        out_shape=[
            jax.ShapeDtypeStruct((rows, width), BF16),
            jax.ShapeDtypeStruct(held.shape, held.dtype),
        ],
        input_output_aliases={3: 0} if more else {},
        cost_estimate=pl.CostEstimate(
            flops=2 * count * tile * width * width,
            bytes_accessed=4 * count * tile * width,
            transcendentals=0,
        ),
        compiler_params=pltpu.CompilerParams(vmem_limit_bytes=GRAD_VMEM),
        name="input_grad",
    )(grads, weight, held, *more)


def activate(half, exact):
    lift = 1.0 + jnp.tanh(half)
    value = half * lift
    if exact:
        return value.astype(BF16), lift + value * (2.0 - lift)
    value, lift = value.astype(BF16), lift.astype(BF16)
    return value, lift + value * (jnp.asarray(2, BF16) - lift)


def layers_kernel(masks, *refs):
    gathered = refs[1:9]
    place_ref = refs[0]
    sources, weight_ref = refs[9:11], refs[11]
    out_hbm, grad_out, wt_a, keep_ref, send_ref = refs[12:17]
    dir_a, dir_b, w_a, w_b, wt_b, gw_a, gw_b, vec, gsum, landed, columns, arrived = refs[17:29]
    held, leaving, came, left = refs[29:31], refs[31:33], refs[33], refs[34]
    tile, width = held[0].shape[1:]
    total = sources[0].shape[0]
    first = total % tile or tile
    count = (total - first) // tile

    def fetches(start, size, place):
        return [
            pltpu.make_async_copy(
                source.at[pl.ds(start, size), :],
                ref.at[place, pl.ds(0, size), :],
                came.at[k, place],
            )
            for k, (source, ref) in enumerate(zip(sources, held))
        ]

    def leaves(start, size, place):
        return [
            pltpu.make_async_copy(
                ref.at[place, pl.ds(0, size), :],
                target.at[pl.ds(start, size), :],
                left.at[k, place],
            )
            for k, (ref, target) in enumerate(zip(leaving, (out_hbm, grad_out)))
        ]

    def start_of(index):
        return pl.multiple_of(first + (index - 1) * tile, SLOT)

    def begin(copies):
        for copy in copies:
            copy.start()

    def finish(copies):
        for copy in copies:
            copy.wait()

    begin(fetches(0, first, 0))

    def owner(slot):
        return place_ref[0] ^ masks[slot]

    copies = [
        pltpu.make_async_copy(ref, landed.at[k], arrived.at[k])
        for k, ref in enumerate(gathered)
    ]
    for copy in copies:
        copy.start()
    for copy in copies:
        copy.wait()
    squares = [jnp.zeros((SLOT, width), F32)] * 2
    for slot in range(len(masks)):
        rows = pl.ds(pl.multiple_of(owner(slot) * SLOT, SLOT), SLOT)
        for k, direction in enumerate((dir_a, dir_b)):
            block = landed[slot // 4, slot % 4, :, k * width : (k + 1) * width]
            direction[rows, :] = block
            squares[k] = squares[k] + block.astype(F32) * block.astype(F32)
        columns[rows, :] = landed[slot // 4, slot % 4, :, 2 * width :].astype(F32)
    small = columns[...].T
    for k, (direction, w) in enumerate(((dir_a, w_a), (dir_b, w_b))):
        norm = lax.rsqrt(jnp.sum(squares[k], axis=0, keepdims=True) + EPS)
        scale = small[2 * k : 2 * k + 1] * norm
        for row in range(0, width, STRIP):
            strip = slice(row, row + STRIP)
            weight = (scale * direction[strip, :].astype(F32)).astype(BF16)
            w[strip, :] = weight * jnp.asarray(0.5, BF16)
            if k == 0:
                wt_a[strip, :] = weight
        vec[3 * k : 3 * k + 1, :] = 0.5 * small[2 * k + 1 : 2 * k + 2]
        vec[3 * k + 1 : 3 * k + 2, :] = scale
        vec[3 * k + 2 : 3 * k + 3, :] = norm
    wt_b[...] = w_b[...].T

    join = lambda pieces: jnp.concatenate(pieces, axis=0)

    def work(line, size, place, fresh):
        x_ref, cot_ref, out_ref, grad_ref = [ref.at[place] for ref in (*held, *leaving)]
        whole = pl.ds(0, size)
        spans = [pl.ds(k, min(PART, size - k)) for k in range(0, size, PART)]
        hidden, slope_a = zip(
            *[activate(dot(x_ref[s, :], w_a[...]) + vec[0:1, :], True) for s in spans]
        )
        slope_a = [v.astype(BF16) for v in slope_a]
        grads = []
        for s, h in zip(spans, hidden):
            value, slope_b = activate(dot(h, w_b[...]) + vec[3:4, :], True)
            out_ref[s, :] = value
            rows = [
                jnp.broadcast_to(weight_ref[pl.ds(line + k, 1), :], (LANES, LANES))
                for k in range(s.start // LANES, (s.start + s.size) // LANES)
            ]
            weight = join([row.T for row in rows])
            weight = jnp.concatenate([weight] * (width // LANES), axis=1)
            grads.append(cot_ref[s, :] * (weight * slope_b).astype(BF16))
        grads_a = [
            (dot(g, wt_b[...]) * sa.astype(F32)).astype(BF16) for g, sa in zip(grads, slope_a)
        ]
        for s, g in zip(spans, grads_a):
            grad_ref[s, :] = g
        ones = jnp.ones((SLOT, size), BF16)
        add = lambda ref, part: part if fresh else ref + part
        gw_b[...] = add(gw_b[...], dot(join([join(hidden).T, ones]), join(grads)))
        gw_a[...] = add(gw_a[...], dot(join([x_ref[whole, :].T, ones]), grad_ref[whole, :]))

    if count:
        begin(fetches(start_of(1), tile, 1))
    finish(fetches(0, first, 0))
    work(0, first, 0, True)
    begin(leaves(0, first, 0))

    def turn(index, carry):
        place = lax.rem(index, 2)

        @pl.when(index < count)
        def _():
            begin(fetches(start_of(index + 1), tile, 1 - place))

        @pl.when(index == 2)
        def _():
            finish(leaves(0, first, 0))

        @pl.when(index > 2)
        def _():
            finish(leaves(start_of(index - 2), tile, place))

        finish(fetches(start_of(index), tile, place))
        work(start_of(index) // LANES, tile, place, False)
        begin(leaves(start_of(index), tile, place))
        return carry

    lax.fori_loop(1, count + 1, turn, 0)

    small, factors = [], []
    for k, (direction, gw) in enumerate(((dir_a, gw_a), (dir_b, gw_b))):
        inner = jnp.zeros((8, width), F32)
        for row in range(0, width, STRIP):
            product = gw[row : row + STRIP, :] * direction[row : row + STRIP, :].astype(F32)
            inner = inner + jnp.sum(product.reshape(STRIP // 8, 8, width), axis=0)
        inner = jnp.sum(inner, axis=0, keepdims=True)
        scale, norm = vec[3 * k + 1 : 3 * k + 2, :], vec[3 * k + 2 : 3 * k + 3, :]
        small += [norm * inner, gw[width : width + 1, :]]
        factors.append((scale, scale * norm * norm * inner))
    gsum[...] = jnp.concatenate(small + [jnp.zeros((4, width), F32)], axis=0)
    for slot in range(len(masks)):
        home = owner(slot)
        rows = pl.ds(pl.multiple_of(home * SLOT, SLOT), SLOT)
        chunk = pl.ds(pl.multiple_of(home * SLOT // LANES * LANES, LANES), LANES)
        extra = pltpu.roll(gsum[:, chunk], LANES - home * SLOT % LANES, 1)
        pieces = [
            scale * gw[rows, :] - other * direction[rows, :].astype(F32)
            for (scale, other), direction, gw in zip(factors, (dir_a, dir_b), (gw_a, gw_b))
        ]
        pieces.append(jnp.concatenate([extra, jnp.zeros((8, LANES), F32)], axis=0))
        block = jnp.concatenate(pieces, axis=1)
        if slot < len(masks) // 2:
            keep_ref[slot] = block
        else:
            send_ref[slot - len(masks) // 2] = block.astype(BF16)

    if count < 2:
        finish(leaves(0, first, 0))
    for index in range(max(1, count - 1), count + 1):
        finish(leaves(start_of(index), tile, index % 2))


def layers(place, gathered, layer_input, cotangent, weights, masks):
    rows, width = layer_input.shape
    tile = min(BIG_TILE, rows)
    span = 2 * width + LANES
    half = len(masks) // 2
    square = lambda dtype: pltpu.VMEM((width, width), dtype)
    return pl.pallas_call(
        functools.partial(layers_kernel, masks),
        in_specs=[pl.BlockSpec(memory_space=pltpu.SMEM)]
        + [pl.BlockSpec(memory_space=pl.ANY)] * 8
        + [pl.BlockSpec(memory_space=pl.ANY)] * 2
        + [pl.BlockSpec(memory_space=pltpu.VMEM)],
        out_specs=[
            pl.BlockSpec(memory_space=pl.ANY),
            pl.BlockSpec(memory_space=pl.ANY),
            pl.BlockSpec(memory_space=pltpu.VMEM),
            pl.BlockSpec(memory_space=pltpu.VMEM),
            pl.BlockSpec(memory_space=pltpu.VMEM),
        ],
        out_shape=[
            jax.ShapeDtypeStruct((rows, width), BF16),
            pltpu.VMEM((rows, width), BF16),
            jax.ShapeDtypeStruct((width, width), BF16),
            jax.ShapeDtypeStruct((half, SLOT, span), F32),
            jax.ShapeDtypeStruct((half, SLOT, span), BF16),
        ],
        scratch_shapes=[square(BF16)] * 5
        + [pltpu.VMEM((width + SLOT, width), F32)] * 2
        + [
            pltpu.VMEM((8, width), F32),
            pltpu.VMEM((8, width), F32),
            pltpu.VMEM((8, 4, SLOT, span), BF16),
            pltpu.VMEM((width, LANES), F32),
            pltpu.SemaphoreType.DMA((8,)),
            pltpu.VMEM((2, tile, width), BF16),
            pltpu.VMEM((2, tile, width), BF16),
            pltpu.VMEM((2, tile, width), BF16),
            pltpu.VMEM((2, tile, width), BF16),
            pltpu.SemaphoreType.DMA((2, 2)),
            pltpu.SemaphoreType.DMA((2, 2)),
        ],
        compiler_params=pltpu.CompilerParams(vmem_limit_bytes=VMEM_BYTES),
        name="layers",
    )(place, *gathered, layer_input, cotangent, weights)


def swap(value, mask, groups):
    return lax.ppermute(value, AXES, [(k, k ^ mask) for k in range(groups)])


def body(
    layer_input,
    cotangent,
    shape_points,
    shape_category,
    category_counts,
    dir_a,
    gain_a,
    bias_a,
    dir_b,
    gain_b,
    bias_b,
):
    dp, fsdp = lax.axis_size("dp"), lax.axis_size("fsdp")
    groups = dp * fsdp
    rows, width = layer_input.shape
    share = dir_a.shape[0]
    slots = width // SLOT
    average = groups * rows // shape_points.shape[0]
    me = lax.axis_index(AXES).astype(jnp.int32)
    fast = share == SLOT and groups == 32 and fsdp == 8
    small = jnp.stack([gain_a, bias_a, gain_b, bias_b])
    place = jnp.stack([me if fast else jnp.zeros_like(me), me * rows])
    weigh = lambda held: point_weights(
        place, shape_points, shape_category, category_counts, held, rows, average
    )
    if fast:
        span = 2 * width + LANES
        lane = lax.broadcasted_iota(jnp.int32, (share, span), 1)
        mine = jnp.pad(dir_a, ((0, 0), (0, span - width)))
        late = jnp.pad(dir_b, ((0, 0), (width, span - 2 * width)))
        mine = jnp.where(lane < width, mine, late)
        for k, vector in enumerate((gain_a, bias_a, gain_b, bias_b)):
            mine = jnp.where(lane == 2 * width + k, vector[:, None], mine)
        mine = mine[None]
        near = [mine] + [swap(mine, m, groups) for m in (2, 4, 6)]
        near = jnp.concatenate(near, axis=0)
        weights, same = weigh(near)
        wide = [same] + [swap(near, m, groups) for m in (1, 16, 17)]
        gathered = wide + [swap(v, 8, groups) for v in wide]
        masks = [c ^ xy ^ z for c in (0, 8) for xy in (0, 1, 16, 17) for z in (0, 2, 4, 6)]
    else:
        full = [lax.all_gather(v, AXES, axis=0, tiled=True) for v in (dir_a, dir_b)]
        vectors = lax.all_gather(small, AXES, axis=1, tiled=True)
        extra = jnp.pad(vectors.T.reshape(slots, SLOT, 4), ((0, 0), (0, 0), (0, LANES - 4)))
        blocks = [v.reshape(slots, SLOT, width) for v in full] + [extra]
        blocks = jnp.concatenate(blocks, axis=2)
        gathered = [blocks[4 * k : 4 * k + 4] for k in range(8)]
        masks = list(range(slots))
        weights, _ = weigh(dir_a)
    tile = pick_tile(rows)
    tiles = rows // tile
    first = tiles * 5 // 8
    layer_output, grads, weight, keep, send = layers(
        place, gathered, layer_input, cotangent, weights, masks
    )
    if fast:
        total = keep + swap(send, 8, groups).astype(F32)
        parts = [total[4 * k : 4 * k + 4] for k in range(4)]
        came = [swap(parts[k].astype(BF16), m, groups) for k, m in ((1, 1), (2, 16), (3, 17))]
        input_grad, held = input_grads(grads, weight, parts[0], None, tile, 0, first)
        total = held + sum(v.astype(F32) for v in came)
        came = [swap(total[k].astype(BF16), m, groups) for k, m in ((1, 2), (2, 4), (3, 6))]
        input_grad, held = input_grads(
            grads, weight, total[0], input_grad, tile, first, tiles - first
        )
        total = held + sum(v.astype(F32) for v in came)
        vectors = total[0:4, 2 * width : 2 * width + SLOT]
        grad_a, grad_b = total[:, :width], total[:, width : 2 * width]
    else:
        input_grad, _ = input_grads(grads, weight, keep[0], None, tile, 0, tiles)
        total = jnp.concatenate([keep, send.astype(F32)], axis=0)
        scatter = lambda v, d: lax.psum_scatter(v, AXES, scatter_dimension=d, tiled=True)
        square = total[:, :, : 2 * width].reshape(width, 2 * width)
        square = scatter(square, 0)
        grad_a, grad_b = square[:, :width], square[:, width:]
        vectors = total[:, 0:4, 2 * width : 2 * width + SLOT].transpose(1, 0, 2).reshape(4, width)
        vectors = scatter(vectors, 1)
    return (
        layer_output,
        input_grad,
        grad_a,
        vectors[0],
        vectors[1],
        grad_b,
        vectors[2],
        vectors[3],
    )


def solution(mesh):
    rows, row, none = P(AXES, None), P(AXES), P()
    in_specs = (rows, rows, none, none, none, rows, row, row, rows, row, row)
    out_specs = (rows, rows, rows, row, row, rows, row, row)
    return jax.shard_map(body, mesh=mesh, in_specs=in_specs, out_specs=out_specs, check_vma=False)
```

```python
import functools
import math

import jax
import jax.numpy as jnp
from jax import lax
from jax.experimental import pallas as pl
from jax.experimental.pallas import tpu as pltpu
from jax.sharding import PartitionSpec as P

AXES = ("dp", "fsdp")
EPS = 1e-06
SLOT = 16
LANES = 128
F32 = jnp.float32
BF16 = jnp.bfloat16
VMEM_BYTES = 36 << 20
BIG_TILE = 1792
PART = 256
STRIP = 64
GRAD_VMEM = 10 << 20


def pick_tile(rows):
    for tile in (1472, 736, 512, 368, 256, 128, 64, 32, 16):
        if rows % tile == 0:
            return tile
    return rows


def dot(left, right):
    return jnp.dot(left, right, preferred_element_type=F32)


def point_weight_kernel(average, place_ref, counts_ref, points_ref, category_ref, mine_ref, out_ref, same_ref):
    same_ref[...] = mine_ref[...]
    line = lax.broadcasted_iota(jnp.int32, out_ref.shape, 0)
    position = place_ref[1] + line * LANES + lax.broadcasted_iota(jnp.int32, out_ref.shape, 1)

    def enter(shape, carry):
        start, count, points = carry
        after = position >= start
        count = jnp.where(after, counts_ref[category_ref[shape]], count)
        points = jnp.where(after, points_ref[shape], points)
        return start + points_ref[shape], count, points

    zero = jnp.zeros(out_ref.shape, jnp.int32)
    shapes = points_ref.shape[0]
    _, count, points = lax.fori_loop(
        0, shapes, enter, (jnp.int32(0), zero, zero), unroll=math.gcd(shapes, 8)
    )
    out_ref[...] = (
        count.astype(F32) * (average / 8.0) / jnp.maximum(points, average // 2).astype(F32)
    )


def point_weights(place, shape_points, shape_category, category_counts, mine, rows, average):
    lines = -(-rows // LANES // 8) * 8
    return pl.pallas_call(
        functools.partial(point_weight_kernel, average),
        in_specs=[pl.BlockSpec(memory_space=pltpu.SMEM)] * 4
        + [pl.BlockSpec(memory_space=pltpu.VMEM)],
        out_specs=[pl.BlockSpec(memory_space=pltpu.VMEM)] * 2,
        out_shape=[
            jax.ShapeDtypeStruct((lines, LANES), F32),
            jax.ShapeDtypeStruct(mine.shape, mine.dtype),
        ],
        compiler_params=pltpu.CompilerParams(vmem_limit_bytes=8 << 20),
        cost_estimate=pl.CostEstimate(
            flops=50 * rows * LANES, bytes_accessed=2 * rows * LANES, transcendentals=0
        ),
        name="point_weight",
    )(place, category_counts, shape_points, shape_category, mine)


def input_grad_kernel(grad_ref, w_ref, held_ref, *refs):
    out_ref, same_ref = refs[-2:]

    @pl.when(pl.program_id(0) == 0)
    def _():
        same_ref[...] = held_ref[...]

    out_ref[...] = lax.dot_general(
        grad_ref[...], w_ref[...], (((1,), (1,)), ((), ())), preferred_element_type=F32
    ).astype(BF16)


def input_grads(grads, weight, held, whole, tile, first, count):
    rows, width = grads.shape
    by_row = pl.BlockSpec((tile, width), lambda i: (i + first, 0))
    every = pl.BlockSpec(held.shape, lambda i: (0,) * held.ndim)
    more = [] if whole is None else [whole]
    return pl.pallas_call(
        input_grad_kernel,
        grid=(count,),
        in_specs=[by_row, pl.BlockSpec((width, width), lambda i: (0, 0)), every]
        + [pl.BlockSpec(memory_space=pl.ANY)] * len(more),
        out_specs=[by_row, every],
        out_shape=[
            jax.ShapeDtypeStruct((rows, width), BF16),
            jax.ShapeDtypeStruct(held.shape, held.dtype),
        ],
        input_output_aliases={3: 0} if more else {},
        cost_estimate=pl.CostEstimate(
            flops=2 * count * tile * width * width,
            bytes_accessed=4 * count * tile * width,
            transcendentals=0,
        ),
        compiler_params=pltpu.CompilerParams(vmem_limit_bytes=GRAD_VMEM),
        name="input_grad",
    )(grads, weight, held, *more)


def activate(half, exact):
    lift = 1.0 + jnp.tanh(half)
    value = half * lift
    if exact:
        return value.astype(BF16), lift + value * (2.0 - lift)
    value, lift = value.astype(BF16), lift.astype(BF16)
    return value, lift + value * (jnp.asarray(2, BF16) - lift)


def layers_kernel(masks, *refs):
    gathered = refs[1:9]
    place_ref = refs[0]
    sources, weight_ref = refs[9:11], refs[11]
    out_hbm, grad_out, wt_a, keep_ref, send_ref = refs[12:17]
    dir_a, dir_b, w_a, w_b, wt_b, gw_a, gw_b, vec, gsum, landed, columns, arrived = refs[17:29]
    held, leaving, came, left = refs[29:31], refs[31:33], refs[33], refs[34]
    tile, width = held[0].shape[1:]
    total = sources[0].shape[0]
    first = total % tile or tile
    count = (total - first) // tile

    def fetches(start, size, place):
        return [
            pltpu.make_async_copy(
                source.at[pl.ds(start, size), :],
                ref.at[place, pl.ds(0, size), :],
                came.at[k, place],
            )
            for k, (source, ref) in enumerate(zip(sources, held))
        ]

    def leaves(start, size, place):
        return [
            pltpu.make_async_copy(
                ref.at[place, pl.ds(0, size), :],
                target.at[pl.ds(start, size), :],
                left.at[k, place],
            )
            for k, (ref, target) in enumerate(zip(leaving, (out_hbm, grad_out)))
        ]

    def start_of(index):
        return pl.multiple_of(first + (index - 1) * tile, SLOT)

    def begin(copies):
        for copy in copies:
            copy.start()

    def finish(copies):
        for copy in copies:
            copy.wait()

    begin(fetches(0, first, 0))

    def owner(slot):
        return place_ref[0] ^ masks[slot]

    copies = [
        pltpu.make_async_copy(ref, landed.at[k], arrived.at[k])
        for k, ref in enumerate(gathered)
    ]
    for copy in copies:
        copy.start()
    for copy in copies:
        copy.wait()
    squares = [jnp.zeros((SLOT, width), F32)] * 2
    for slot in range(len(masks)):
        rows = pl.ds(pl.multiple_of(owner(slot) * SLOT, SLOT), SLOT)
        for k, direction in enumerate((dir_a, dir_b)):
            block = landed[slot // 4, slot % 4, :, k * width : (k + 1) * width]
            direction[rows, :] = block
            squares[k] = squares[k] + block.astype(F32) * block.astype(F32)
        columns[rows, :] = landed[slot // 4, slot % 4, :, 2 * width :].astype(F32)
    small = columns[...].T
    for k, (direction, w) in enumerate(((dir_a, w_a), (dir_b, w_b))):
        norm = lax.rsqrt(jnp.sum(squares[k], axis=0, keepdims=True) + EPS)
        scale = small[2 * k : 2 * k + 1] * norm
        for row in range(0, width, STRIP):
            strip = slice(row, row + STRIP)
            weight = (scale * direction[strip, :].astype(F32)).astype(BF16)
            w[strip, :] = weight * jnp.asarray(0.5, BF16)
            if k == 0:
                wt_a[strip, :] = weight
        vec[3 * k : 3 * k + 1, :] = 0.5 * small[2 * k + 1 : 2 * k + 2]
        vec[3 * k + 1 : 3 * k + 2, :] = scale
        vec[3 * k + 2 : 3 * k + 3, :] = norm
    wt_b[...] = w_b[...].T

    join = lambda pieces: jnp.concatenate(pieces, axis=0)

    def work(line, size, place, fresh):
        x_ref, cot_ref, out_ref, grad_ref = [ref.at[place] for ref in (*held, *leaving)]
        whole = pl.ds(0, size)
        spans = [pl.ds(k, min(PART, size - k)) for k in range(0, size, PART)]
        hidden, slope_a = zip(
            *[activate(dot(x_ref[s, :], w_a[...]) + vec[0:1, :], True) for s in spans]
        )
        slope_a = [v.astype(BF16) for v in slope_a]
        grads = []
        for s, h in zip(spans, hidden):
            value, slope_b = activate(dot(h, w_b[...]) + vec[3:4, :], True)
            out_ref[s, :] = value
            rows = [
                jnp.broadcast_to(weight_ref[pl.ds(line + k, 1), :], (LANES, LANES))
                for k in range(s.start // LANES, (s.start + s.size) // LANES)
            ]
            weight = join([row.T for row in rows])
            weight = jnp.concatenate([weight] * (width // LANES), axis=1)
            grads.append(cot_ref[s, :] * (weight * slope_b).astype(BF16))
        grads_a = [
            (dot(g, wt_b[...]) * sa.astype(F32)).astype(BF16) for g, sa in zip(grads, slope_a)
        ]
        for s, g in zip(spans, grads_a):
            grad_ref[s, :] = g
        ones = jnp.ones((SLOT, size), BF16)
        add = lambda ref, part: part if fresh else ref + part
        gw_b[...] = add(gw_b[...], dot(join([join(hidden).T, ones]), join(grads)))
        gw_a[...] = add(gw_a[...], dot(join([x_ref[whole, :].T, ones]), grad_ref[whole, :]))

    if count:
        begin(fetches(start_of(1), tile, 1))
    finish(fetches(0, first, 0))
    work(0, first, 0, True)
    begin(leaves(0, first, 0))

    def turn(index, carry):
        place = lax.rem(index, 2)

        @pl.when(index < count)
        def _():
            begin(fetches(start_of(index + 1), tile, 1 - place))

        @pl.when(index == 2)
        def _():
            finish(leaves(0, first, 0))

        @pl.when(index > 2)
        def _():
            finish(leaves(start_of(index - 2), tile, place))

        finish(fetches(start_of(index), tile, place))
        work(start_of(index) // LANES, tile, place, False)
        begin(leaves(start_of(index), tile, place))
        return carry

    lax.fori_loop(1, count + 1, turn, 0)

    small, factors = [], []
    for k, (direction, gw) in enumerate(((dir_a, gw_a), (dir_b, gw_b))):
        inner = jnp.zeros((8, width), F32)
        for row in range(0, width, STRIP):
            product = gw[row : row + STRIP, :] * direction[row : row + STRIP, :].astype(F32)
            inner = inner + jnp.sum(product.reshape(STRIP // 8, 8, width), axis=0)
        inner = jnp.sum(inner, axis=0, keepdims=True)
        scale, norm = vec[3 * k + 1 : 3 * k + 2, :], vec[3 * k + 2 : 3 * k + 3, :]
        small += [norm * inner, gw[width : width + 1, :]]
        factors.append((scale, scale * norm * norm * inner))
    gsum[...] = jnp.concatenate(small + [jnp.zeros((4, width), F32)], axis=0)
    for slot in range(len(masks)):
        home = owner(slot)
        rows = pl.ds(pl.multiple_of(home * SLOT, SLOT), SLOT)
        chunk = pl.ds(pl.multiple_of(home * SLOT // LANES * LANES, LANES), LANES)
        extra = pltpu.roll(gsum[:, chunk], LANES - home * SLOT % LANES, 1)
        pieces = [
            scale * gw[rows, :] - other * direction[rows, :].astype(F32)
            for (scale, other), direction, gw in zip(factors, (dir_a, dir_b), (gw_a, gw_b))
        ]
        pieces.append(jnp.concatenate([extra, jnp.zeros((8, LANES), F32)], axis=0))
        block = jnp.concatenate(pieces, axis=1)
        if slot < len(masks) // 2:
            keep_ref[slot] = block
        else:
            send_ref[slot - len(masks) // 2] = block.astype(BF16)

    if count < 2:
        finish(leaves(0, first, 0))
    for index in range(max(1, count - 1), count + 1):
        finish(leaves(start_of(index), tile, index % 2))


def layers(place, gathered, layer_input, cotangent, weights, masks):
    rows, width = layer_input.shape
    tile = min(BIG_TILE, rows)
    span = 2 * width + LANES
    half = len(masks) // 2
    square = lambda dtype: pltpu.VMEM((width, width), dtype)
    return pl.pallas_call(
        functools.partial(layers_kernel, masks),
        in_specs=[pl.BlockSpec(memory_space=pltpu.SMEM)]
        + [pl.BlockSpec(memory_space=pl.ANY)] * 8
        + [pl.BlockSpec(memory_space=pl.ANY)] * 2
        + [pl.BlockSpec(memory_space=pltpu.VMEM)],
        out_specs=[
            pl.BlockSpec(memory_space=pl.ANY),
            pl.BlockSpec(memory_space=pl.ANY),
            pl.BlockSpec(memory_space=pltpu.VMEM),
            pl.BlockSpec(memory_space=pltpu.VMEM),
            pl.BlockSpec(memory_space=pltpu.VMEM),
        ],
        out_shape=[
            jax.ShapeDtypeStruct((rows, width), BF16),
            pltpu.VMEM((rows, width), BF16),
            jax.ShapeDtypeStruct((width, width), BF16),
            jax.ShapeDtypeStruct((half, SLOT, span), F32),
            jax.ShapeDtypeStruct((half, SLOT, span), BF16),
        ],
        scratch_shapes=[square(BF16)] * 5
        + [pltpu.VMEM((width + SLOT, width), F32)] * 2
        + [
            pltpu.VMEM((8, width), F32),
            pltpu.VMEM((8, width), F32),
            pltpu.VMEM((8, 4, SLOT, span), BF16),
            pltpu.VMEM((width, LANES), F32),
            pltpu.SemaphoreType.DMA((8,)),
            pltpu.VMEM((2, tile, width), BF16),
            pltpu.VMEM((2, tile, width), BF16),
            pltpu.VMEM((2, tile, width), BF16),
            pltpu.VMEM((2, tile, width), BF16),
            pltpu.SemaphoreType.DMA((2, 2)),
            pltpu.SemaphoreType.DMA((2, 2)),
        ],
        compiler_params=pltpu.CompilerParams(vmem_limit_bytes=VMEM_BYTES),
        name="layers",
    )(place, *gathered, layer_input, cotangent, weights)


def last_kernel(*refs):
    total = refs[0][...]
    for ref in refs[1:4]:
        total = total + ref[...].astype(F32)
    width = refs[4].shape[1]
    refs[4][...] = total[:, 0:width]
    refs[5][...] = total[:, width : 2 * width]
    for k, ref in enumerate(refs[6:]):
        ref[...] = total[k, 2 * width : 2 * width + SLOT]


def add_last(held, came, width):
    square = jax.ShapeDtypeStruct((SLOT, width), F32)
    vector = jax.ShapeDtypeStruct((SLOT,), F32)
    return pl.pallas_call(
        last_kernel,
        in_specs=[pl.BlockSpec(memory_space=pltpu.VMEM)] * 4,
        out_specs=[pl.BlockSpec(memory_space=pltpu.VMEM)] * 6,
        out_shape=[square, square] + [vector] * 4,
        compiler_params=pltpu.CompilerParams(vmem_limit_bytes=4 << 20),
        name="last",
    )(held, *came)


def swap(value, mask, groups):
    return lax.ppermute(value, AXES, [(k, k ^ mask) for k in range(groups)])


def body(
    layer_input,
    cotangent,
    shape_points,
    shape_category,
    category_counts,
    dir_a,
    gain_a,
    bias_a,
    dir_b,
    gain_b,
    bias_b,
):
    dp, fsdp = lax.axis_size("dp"), lax.axis_size("fsdp")
    groups = dp * fsdp
    rows, width = layer_input.shape
    share = dir_a.shape[0]
    slots = width // SLOT
    average = groups * rows // shape_points.shape[0]
    me = lax.axis_index(AXES).astype(jnp.int32)
    fast = share == SLOT and groups == 32 and fsdp == 8
    small = jnp.stack([gain_a, bias_a, gain_b, bias_b])
    place = jnp.stack([me if fast else jnp.zeros_like(me), me * rows])
    weigh = lambda held: point_weights(
        place, shape_points, shape_category, category_counts, held, rows, average
    )
    if fast:
        span = 2 * width + LANES
        lane = lax.broadcasted_iota(jnp.int32, (share, span), 1)
        mine = jnp.pad(dir_a, ((0, 0), (0, span - width)))
        late = jnp.pad(dir_b, ((0, 0), (width, span - 2 * width)))
        mine = jnp.where(lane < width, mine, late)
        for k, vector in enumerate((gain_a, bias_a, gain_b, bias_b)):
            mine = jnp.where(lane == 2 * width + k, vector[:, None], mine)
        mine = mine[None]
        near = [mine] + [swap(mine, m, groups) for m in (2, 4, 6)]
        near = jnp.concatenate(near, axis=0)
        weights, same = weigh(near)
        wide = [same] + [swap(near, m, groups) for m in (1, 16, 17)]
        gathered = wide + [swap(v, 8, groups) for v in wide]
        masks = [c ^ xy ^ z for c in (0, 8) for xy in (0, 1, 16, 17) for z in (0, 2, 4, 6)]
    else:
        full = [lax.all_gather(v, AXES, axis=0, tiled=True) for v in (dir_a, dir_b)]
        vectors = lax.all_gather(small, AXES, axis=1, tiled=True)
        extra = jnp.pad(vectors.T.reshape(slots, SLOT, 4), ((0, 0), (0, 0), (0, LANES - 4)))
        blocks = [v.reshape(slots, SLOT, width) for v in full] + [extra]
        blocks = jnp.concatenate(blocks, axis=2)
        gathered = [blocks[4 * k : 4 * k + 4] for k in range(8)]
        masks = list(range(slots))
        weights, _ = weigh(dir_a)
    tile = pick_tile(rows)
    tiles = rows // tile
    first = tiles * 5 // 8
    layer_output, grads, weight, keep, send = layers(
        place, gathered, layer_input, cotangent, weights, masks
    )
    if fast:
        total = keep + swap(send, 8, groups).astype(F32)
        parts = [total[4 * k : 4 * k + 4] for k in range(4)]
        came = [swap(parts[k].astype(BF16), m, groups) for k, m in ((1, 1), (2, 16), (3, 17))]
        input_grad, held = input_grads(grads, weight, parts[0], None, tile, 0, first)
        total = held + sum(v.astype(F32) for v in came)
        came = [swap(total[k].astype(BF16), m, groups) for k, m in ((1, 2), (2, 4), (3, 6))]
        input_grad, held = input_grads(
            grads, weight, total[0], input_grad, tile, first, tiles - first
        )
        grad_a, grad_b, *vectors = add_last(held, came, width)
    else:
        input_grad, _ = input_grads(grads, weight, keep[0], None, tile, 0, tiles)
        total = jnp.concatenate([keep, send.astype(F32)], axis=0)
        scatter = lambda v, d: lax.psum_scatter(v, AXES, scatter_dimension=d, tiled=True)
        square = total[:, :, : 2 * width].reshape(width, 2 * width)
        square = scatter(square, 0)
        grad_a, grad_b = square[:, :width], square[:, width:]
        vectors = total[:, 0:4, 2 * width : 2 * width + SLOT].transpose(1, 0, 2).reshape(4, width)
        vectors = scatter(vectors, 1)
    return (
        layer_output,
        input_grad,
        grad_a,
        vectors[0],
        vectors[1],
        grad_b,
        vectors[2],
        vectors[3],
    )


def solution(mesh):
    rows, row, none = P(AXES, None), P(AXES), P()
    in_specs = (rows, rows, none, none, none, rows, row, row, rows, row, row)
    out_specs = (rows, rows, rows, row, row, rows, row, row)
    return jax.shard_map(body, mesh=mesh, in_specs=in_specs, out_specs=out_specs, check_vma=False)
```
